32 devices in a mesh: sec: 2 (over core), tile: 16 (over z, y, x).
Axes of the slice: x: 2, y: 2, z: 4, core: 2. Of those that a mesh axis runs over, the one named last changes fastest.
Arguments:
- displacement: float32 [2, 2, 32, 4096], P('sec', None, 'tile'), may hold values from -6 to 6
- stiffness: float32 [2, 32, 4096], P('sec', 'tile'), may hold values from 0.5 to 2
- match_weight: float32 [2, 48, 512], P('sec', 'tile'), may hold values from 0.5 to 4
- match_offset: float32 [2, 2, 48, 512], P('sec', None, 'tile'), may hold values from -6 to 6
- source_row: int32 [2, 48, 512], P('sec', 'tile'), may hold values from 0 to 1
- source_col: int32 [2, 48, 512], P('sec', 'tile'), may hold values from 0 to 4095
- target_row: int32 [2, 48, 512], P('sec', 'tile'), may hold values from 0 to 1
- target_col: int32 [2, 48, 512], P('sec', 'tile'), may hold values from 0 to 4095
- match_count: int32 [2, 48], P('sec', 'tile'), may hold values from 0 to 512, as said below
Outputs:
- aligned: float32 [2, 2, 32, 4096], P('sec', None, 'tile')
The draws below stay inside these ranges and needn't reach their ends.
Inputs may be any that keep to these rules, and one draw needn't show every extreme that they name: `match_count`: in every section some tile's group 1 uses all 512 slots, and some tile other than the first and the last uses all 512 slots in group 0 and in group 2.
All inputs are finite; a program needn't handle non-finite values.
Results may differ from the reference program's by a relative error of at most 0.0018.
Values sent between devices are 32-bit elements; how exact they have to be, the bound alone decides.
A program may use at most 64 MiB of HBM per device.

```python
import math
import jax
import jax.numpy as jnp
from jax import lax

W = 4096
ROWS_DEV = 2
MATCH = 512
STEPS = 2
SECTIONS = 2
NROWS = 32
N_TILE = 16


def draw_match_count(key, part):
    key_own, key_edge, key_pick, key_side = jax.random.split(jax.random.fold_in(key, 17), 4)
    own = jax.random.randint(key_own, (SECTIONS, N_TILE), MATCH // 4, MATCH + 1)
    edge = jax.random.randint(key_edge, (SECTIONS, N_TILE, 2), MATCH // 8, MATCH + 1)
    picked = jax.random.randint(key_pick, (SECTIONS,), 0, N_TILE)
    side_pick = jax.random.randint(key_side, (SECTIONS,), 1, N_TILE - 1)
    tiles = jnp.arange(N_TILE)
    own = jnp.where(tiles[None, :] == picked[:, None], MATCH, own)
    edge = jnp.where((tiles[None, :] == side_pick[:, None])[..., None], MATCH, edge)
    counts = jnp.stack([edge[..., 0], own, edge[..., 1]], axis=-1)
    return counts.reshape(SECTIONS, 3 * N_TILE).astype(jnp.int32)


def with_ends(entries, own_key, least, largest):
    place = [jax.random.randint(jax.random.fold_in(own_key, axis), (), 0, length) for axis, length in enumerate(entries.shape)]
    widest = entries.shape.index(max(entries.shape))
    next_to = place[:widest] + [(place[widest] + 1) % entries.shape[widest]] + place[widest + 1:]
    return entries.at[tuple(place)].set(least).at[tuple(next_to)].set(largest)


def block_scale(rng, shape, cuts, least, top_value):
    factor_of = 1.0
    for axis_at, shards_of in cuts:
        draws = jax.random.uniform(jax.random.fold_in(jax.random.fold_in(rng, 6), axis_at), (shards_of,), jnp.float32, least / len(cuts), top_value / len(cuts))
        factor_of = factor_of * jnp.repeat(jnp.exp(draws), shape[axis_at] // shards_of).reshape((-1,) + (1,) * (len(shape) - 1 - axis_at))
    return factor_of


def normal_values(key, shape, deviation, bound, cuts=(), kind=jnp.bfloat16):
    result = jax.random.normal(key, shape, jnp.float32) * deviation
    if len(cuts) > 0:
        result = block_scale(key, shape, cuts, -0.22, 0.18) * result
    return jnp.clip(result, min=-bound, max=bound).astype(kind)


def setup_inputs(seed: int = 0) -> dict:
    key_of = jax.random.split(jax.random.key(seed), 10)
    return {
        "displacement": normal_values(key_of[0], (SECTIONS, 2, NROWS, W), 1.0, 6.0, ((0, 2), (2, 16)), jnp.float32),
        "stiffness": jnp.clip(jnp.exp(math.log(2.0) - 1.3862944 * jax.random.uniform(key_of[1], (SECTIONS, NROWS, W), jnp.float32) ** block_scale(key_of[1], (SECTIONS, NROWS, W), ((0, 2), (1, 16)), -0.2, 0.2)), 0.5, 2.0),
        "match_weight": jnp.clip(jnp.exp(math.log(4.0) - 2.0794415 * jax.random.uniform(key_of[2], (SECTIONS, 3 * N_TILE, MATCH), jnp.float32) ** block_scale(key_of[2], (SECTIONS, 3 * N_TILE, MATCH), ((0, 2), (1, 16)), -0.2, 0.2)), 0.5, 4.0),
        "match_offset": normal_values(key_of[3], (SECTIONS, 2, 3 * N_TILE, MATCH), 1.0, 6.0, ((0, 2), (2, 16)), jnp.float32),
        "source_row": with_ends(jax.random.randint(key_of[4], (SECTIONS, 3 * N_TILE, MATCH), 0, ROWS_DEV), jax.random.fold_in(key_of[4], 1), 0, ROWS_DEV - 1).astype(jnp.int32),
        "source_col": with_ends(jax.random.randint(key_of[5], (SECTIONS, 3 * N_TILE, MATCH), 0, W), jax.random.fold_in(key_of[5], 1), 0, W - 1).astype(jnp.int32),
        "target_row": with_ends(jax.random.randint(key_of[6], (SECTIONS, 3 * N_TILE, MATCH), 0, ROWS_DEV), jax.random.fold_in(key_of[6], 1), 0, ROWS_DEV - 1).astype(jnp.int32),
        "target_col": with_ends(jax.random.randint(key_of[7], (SECTIONS, 3 * N_TILE, MATCH), 0, W), jax.random.fold_in(key_of[7], 1), 0, W - 1).astype(jnp.int32),
        "match_count": draw_match_count(jax.random.fold_in(key_of[9], 71), 0),
    }


neighbours = [(-1, 0, 1.0), (1, 0, 1.0), (0, -1, 1.0), (0, 1, 1.0), (-1, -1, 0.5), (-1, 1, 0.5), (1, -1, 0.5), (1, 1, 0.5)]
damping = 0.7


def springs(padded_u, padded_c, field, stiff_now):
    row_count = field.shape[1]
    col_count = field.shape[2]
    force = jnp.zeros_like(field)
    total = jnp.zeros_like(stiff_now)
    for row_shift, col_shift, factor in neighbours:
        near_u = padded_u[:, 1 + row_shift:1 + row_shift + row_count, 1 + col_shift:1 + col_shift + col_count]
        near_c = padded_c[1 + row_shift:1 + row_shift + row_count, 1 + col_shift:1 + col_shift + col_count]
        spring = factor * stiff_now * near_c
        force = force + spring[None] * (near_u - field)
        total = total + spring
    return force, total


def section_springs(pair):
    field, stiff_now = pair
    padded_u = jnp.pad(field, ((0, 0), (1, 1), (1, 1)))
    padded_c = jnp.pad(stiff_now, ((1, 1), (1, 1)))
    return springs(padded_u, padded_c, field, stiff_now)


def reference(displacement, stiffness, match_weight, match_offset, source_row, source_col, target_row, target_col, match_count):
    n_sec = SECTIONS
    n_tile = N_TILE
    slots = MATCH
    sections = jnp.arange(n_sec).astype(jnp.int32)
    tiles = jnp.arange(n_tile).astype(jnp.int32)
    groups = jnp.arange(3).astype(jnp.int32)
    slot_ids = jnp.arange(slots).astype(jnp.int32)
    counts = match_count.reshape(n_sec, n_tile, 3)
    dest_tile = tiles[:, None] + groups[None, :] - 1
    tile_ok = (dest_tile >= 0) & (dest_tile < n_tile)
    usable = (slot_ids[None, None, None, :] < counts[..., None]) & (sections[:, None, None, None] < n_sec - 1) & tile_ok[None, :, :, None]
    weight = jnp.where(usable, match_weight.reshape(n_sec, n_tile, 3, slots), jnp.float32(0.0))
    offset = match_offset.reshape(n_sec, 2, n_tile, 3, slots).transpose(1, 0, 2, 3, 4).reshape(2, -1)
    source_rows = tiles[None, :, None, None] * ROWS_DEV + source_row.reshape(n_sec, n_tile, 3, slots)
    source_idx = ((sections[:, None, None, None] * NROWS + source_rows) * W + source_col.reshape(n_sec, n_tile, 3, slots)).astype(jnp.int32)
    next_sec = jnp.clip(sections + 1, 0, n_sec - 1).astype(jnp.int32)
    dest_clip = jnp.clip(dest_tile, 0, n_tile - 1).astype(jnp.int32)
    recv_slot = (2 - groups).astype(jnp.int32)
    rows_arr = target_row.reshape(n_sec, n_tile, 3, slots)
    cols_arr = target_col.reshape(n_sec, n_tile, 3, slots)
    target_rows = rows_arr[next_sec[:, None, None], dest_clip[None, :, :], recv_slot[None, None, :]]
    target_cols = cols_arr[next_sec[:, None, None], dest_clip[None, :, :], recv_slot[None, None, :]]
    target_idx = ((next_sec[:, None, None, None] * NROWS + dest_clip[None, :, :, None] * ROWS_DEV + target_rows) * W + target_cols).astype(jnp.int32)
    source_idx = source_idx.reshape(-1)
    target_idx = target_idx.reshape(-1)
    weight = weight.reshape(-1)
    flat_u = displacement.transpose(1, 0, 2, 3).reshape(2, -1)
    for sweep_no in range(STEPS):
        fields = flat_u.reshape(2, n_sec, NROWS, W).transpose(1, 0, 2, 3)
        force, total = lax.map(section_springs, (fields, stiffness))
        flat_force = force.transpose(1, 0, 2, 3).reshape(2, -1)
        flat_total = total.reshape(-1)
        pull = weight[None] * (flat_u[:, target_idx] - (flat_u[:, source_idx] - offset))
        flat_force = flat_force.at[:, source_idx].add(pull)
        flat_force = flat_force.at[:, target_idx].add(-pull)
        flat_total = flat_total.at[source_idx].add(weight)
        flat_total = flat_total.at[target_idx].add(weight)
        flat_u = flat_u + damping * flat_force / flat_total[None]
    return flat_u.reshape(2, n_sec, NROWS, W).transpose(1, 0, 2, 3)
```

```python
import functools
import jax
import jax.numpy as jnp
from jax import lax
from jax.experimental import pallas as pl
from jax.experimental.pallas import tpu as pltpu
from jax.sharding import PartitionSpec as P

STEPS = 2
DAMPING = 0.7
LANES = 128
MESH = pl.DeviceIdType.MESH


def stencil(rows, above, below):
    chunks = rows[0].shape[0]
    lane = lax.broadcasted_iota(jnp.int32, rows[0].shape, 1)
    chunk = lax.broadcasted_iota(jnp.int32, rows[0].shape, 0)
    sums = []
    for here, beside in ((rows[0], above + rows[1]), (rows[1], rows[0] + below)):
        both = here + 0.5 * beside
        left = pltpu.roll(both, 1, 1)
        left = jnp.where(lane == 0, jnp.where(chunk == 0, 0.0, pltpu.roll(left, 1, 0)), left)
        right = pltpu.roll(both, LANES - 1, 1)
        right = jnp.where(
            lane == LANES - 1,
            jnp.where(chunk == chunks - 1, 0.0, pltpu.roll(right, chunks - 1, 0)),
            right,
        )
        sums.append(beside + left + right)
    return sums


def two_parts(values):
    high = values.astype(jnp.bfloat16)
    low = (values - high.astype(jnp.float32)).astype(jnp.bfloat16)
    return high, low


def kernel(
    n_sec, n_tile, disp, stiff, wgt, off, srow, scol, trow, tcol, cnt, out,
    field, force, total, inv, lhs, hot_lo, hi_ids, edge, halo, mine, theirs, weights,
    edge_send, edge_recv, val_send, val_recv, wgt_send, wgt_recv,
):
    sec = lax.axis_index("sec")
    tile = lax.axis_index("tile")
    chunks = field.shape[2]
    nodes_hi = 2 * chunks
    slots = wgt.shape[1]
    has_tile = [tile > 0, None, tile < n_tile - 1]
    has_sec = [sec < n_sec - 1, sec > 0]
    sec_of = [sec + 1, sec - 1]
    rows_of = [srow, trow]
    cols_of = [scol, tcol]

    def when_tile(g, body):
        if has_tile[g] is None:
            body()
        else:
            pl.when(has_tile[g])(body)

    barrier = pltpu.get_barrier_semaphore()

    def greet(s, t):
        pl.semaphore_signal(barrier, inc=1, device_id=(s, t), device_id_type=MESH)

    for g in (0, 2):
        when_tile(g, lambda g=g: greet(sec, tile + g - 1))
    for role in range(2):

        @pl.when(has_sec[role])
        def _(role=role):
            for g in (1, 0, 2):
                when_tile(g, lambda g=g: greet(sec_of[role], tile + g - 1))

    low_side = jnp.where(tile > 0, 1, 0)
    high_side = jnp.where(tile < n_tile - 1, 1, 0)
    secs = jnp.where(sec > 0, 1, 0) + jnp.where(sec < n_sec - 1, 1, 0)
    greetings = low_side + high_side + secs * (1 + low_side + high_side)

    def edge_copy(step, side):
        count = 3 if step == 0 else 2
        return pltpu.make_async_remote_copy(
            src_ref=edge.at[step, side, pl.ds(0, count)],
            dst_ref=halo.at[step, 1 - side, pl.ds(0, count)],
            send_sem=edge_send.at[step, side],
            recv_sem=edge_recv.at[step, 1 - side],
            device_id=(sec, tile + 2 * side - 1),
            device_id_type=MESH,
        )

    def edge_landed(step, side):
        count = 3 if step == 0 else 2
        return pltpu.make_async_remote_copy(
            src_ref=edge.at[step, side, pl.ds(0, count)],
            dst_ref=halo.at[step, side, pl.ds(0, count)],
            send_sem=edge_send.at[step, side],
            recv_sem=edge_recv.at[step, side],
            device_id=(sec, tile + 2 * side - 1),
            device_id_type=MESH,
        )

    def value_copy(step, role, g, landed=False):
        to_role, to_g = (role, g) if landed else (1 - role, 2 - g)
        return pltpu.make_async_remote_copy(
            src_ref=mine.at[step, role, g],
            dst_ref=theirs.at[step, to_role, to_g],
            send_sem=val_send.at[step, role, g],
            recv_sem=val_recv.at[step, to_role, to_g],
            device_id=(sec_of[role], tile + g - 1),
            device_id_type=MESH,
        )

    def weight_copy(g, landed=False):
        role = 1 if landed else 0
        to_g = g if landed else 2 - g
        return pltpu.make_async_remote_copy(
            src_ref=weights.at[0, g],
            dst_ref=weights.at[1, to_g],
            send_sem=wgt_send.at[g],
            recv_sem=wgt_recv.at[to_g],
            device_id=(sec_of[role], tile + g - 1),
            device_id_type=MESH,
        )

    for r in range(2):
        c_row = stiff[pl.ds(r, chunks, stride=2), :]
        edge[0, r, 2] = c_row
        for k in range(2):
            u_row = disp[k, pl.ds(r, chunks, stride=2), :]
            field[k, r] = u_row
            edge[0, r, k] = c_row * u_row

    for g, side in ((0, 0), (2, 1)):

        @pl.when(jnp.logical_not(has_tile[g]))
        def _(g=g, side=side):
            halo[:, side] = jnp.zeros((STEPS,) + halo.shape[2:], jnp.float32)
            for role in range(2):
                weights[role, g] = jnp.zeros(weights.shape[2:], jnp.float32)
                for step in range(STEPS):
                    theirs[step, role, g] = jnp.zeros(theirs.shape[3:], jnp.float32)

    lane_slot = lax.broadcasted_iota(jnp.int32, (1, slots), 1)

    @pl.when(has_sec[0])
    def _():
        for g in range(3):

            def mask(g=g):
                weights[0, g] = jnp.where(lane_slot < cnt[0, g], wgt[pl.ds(g, 1), :], 0.0)

            when_tile(g, mask)

    lo_node = lax.broadcasted_iota(jnp.int32, (LANES, slots), 0)
    hi_node = lax.broadcasted_iota(jnp.int32, (nodes_hi, slots), 0)

    for role in range(2):

        @pl.when(has_sec[role])
        def _(role=role):
            for g in range(3):
                col = cols_of[role][pl.ds(g, 1), :]
                hi_ids[role, pl.ds(g, 1), :] = rows_of[role][pl.ds(g, 1), :] * chunks + (col >> 7)
                hot = jnp.where(lo_node == (col & (LANES - 1)), 1.0, 0.0).astype(jnp.bfloat16)
                hot_lo[role, pl.ds(0, LANES), pl.ds(g * slots, slots)] = hot
                hot_lo[role, pl.ds(LANES, LANES), pl.ds(g * slots, slots)] = hot

    def hi_mask(role, g):
        return hi_node == hi_ids[role, pl.ds(g, 1), :]

    def pick(step, role):
        for g in (0, 2, 1):
            found = jnp.dot(
                lhs[...],
                hot_lo[role, :, pl.ds(g * slots, slots)],
                preferred_element_type=jnp.float32,
            )
            hit = hi_mask(role, g)
            for k in range(2):
                value = jnp.sum(
                    jnp.where(hit, found[k * nodes_hi : (k + 1) * nodes_hi], 0.0),
                    axis=0,
                    keepdims=True,
                )
                if role == 0:
                    value = value - off[k, pl.ds(g, 1), :]
                mine[step, role, g, pl.ds(k, 1), :] = value

    def spread(role, g, values):
        hot_hi = jnp.where(hi_mask(role, g), 1.0, 0.0)
        parts = []
        for row in values:
            high = row.astype(jnp.bfloat16).astype(jnp.float32)
            parts.append((high, row - high))
        stacked = [(hot_hi * part[i]).astype(jnp.bfloat16) for i in range(2) for part in parts]
        summed = lax.dot_general(
            jnp.concatenate(stacked, axis=0),
            hot_lo[role, pl.ds(0, LANES), pl.ds(g * slots, slots)],
            (((1,), (1,)), ((), ())),
            preferred_element_type=jnp.float32,
        )
        half = len(values) * nodes_hi
        return summed[:half] + summed[half:]

    for step in range(STEPS):
        parts = [two_parts(field[k].reshape(nodes_hi, LANES)) for k in range(2)]
        for k in range(2):
            lhs[pl.ds(k * nodes_hi, nodes_hi), pl.ds(0, LANES)] = parts[k][0]
            lhs[pl.ds(k * nodes_hi, nodes_hi), pl.ds(LANES, LANES)] = parts[k][1]
        if step == 0:
            pl.semaphore_wait(barrier, greetings)
        for g, side in ((0, 0), (2, 1)):
            pl.when(has_tile[g])(lambda side=side: edge_copy(step, side).start())
        if step == 0:

            @pl.when(has_sec[0])
            def _():
                for g in (0, 2, 1):
                    when_tile(g, lambda g=g: weight_copy(g).start())

        for role in range(2):

            @pl.when(has_sec[role])
            def _(role=role):
                pick(step, role)
                for g in (0, 2, 1):
                    when_tile(g, lambda g=g: value_copy(step, role, g).start())

        for g, side in ((0, 0), (2, 1)):
            pl.when(has_tile[g])(lambda side=side: edge_landed(step, side).wait_recv())
        if step == 0:
            rows = [edge[0, r, 2] for r in range(2)]
            sums = stencil(rows, halo[0, 0, 2], halo[0, 1, 2])
            for r in range(2):
                total[r] = rows[r] * sums[r]
        for k in range(2):
            sums = stencil([edge[step, r, k] for r in range(2)], halo[step, 0, k], halo[step, 1, k])
            for r in range(2):
                force[k, r] = edge[0, r, 2] * sums[r] - field[k, r] * total[r]

        if step == 0:
            inv[...] = total[...]
            for role in range(2):

                @pl.when(has_sec[role])
                def _(role=role):
                    for g in range(3):
                        if role == 1:
                            when_tile(g, lambda g=g: weight_copy(g, True).wait_recv())
                        at = spread(role, g, [weights[role, g]])
                        inv[...] += at.reshape(inv.shape)

            inv[...] = DAMPING / inv[...]

        for role in range(2):

            @pl.when(has_sec[role])
            def _(role=role):
                for g in (1, 0, 2):
                    when_tile(g, lambda g=g: value_copy(step, role, g, True).wait_recv())
                    pull = weights[role, g] * (theirs[step, role, g] - mine[step, role, g])
                    at = spread(role, g, [pull[0:1], pull[1:2]])
                    force[...] += at.reshape(force.shape)

        for k in range(2):
            for r in range(2):
                new = field[k, r] + force[k, r] * inv[r]
                if step < STEPS - 1:
                    field[k, r] = new
                    edge[step + 1, r, k] = edge[0, r, 2] * new
                else:
                    out[k, pl.ds(r, chunks, stride=2), :] = new

    for step in range(STEPS):
        for g, side in ((0, 0), (2, 1)):
            pl.when(has_tile[g])(lambda side=side: edge_copy(step, side).wait_send())
        for role in range(2):

            @pl.when(has_sec[role])
            def _(role=role):
                for g in range(3):
                    when_tile(g, lambda g=g: value_copy(step, role, g).wait_send())
                    if step == 0 and role == 0:
                        when_tile(g, lambda g=g: weight_copy(g).wait_send())


def relax(n_sec, n_tile, *args):
    displacement, stiffness, weight, offset, srow, scol, trow, tcol, count = args
    rows, width = stiffness.shape[1:]
    slots = weight.shape[2]
    chunks = width // LANES
    nodes_hi = rows * chunks

    def interleaved(x):
        x = x.reshape(-1, rows, chunks, LANES).transpose(0, 2, 1, 3)
        return x.reshape(-1, nodes_hi, LANES)

    vmem = pl.BlockSpec(memory_space=pltpu.VMEM)
    dma = pltpu.SemaphoreType.DMA
    out = pl.pallas_call(
        functools.partial(kernel, n_sec, n_tile),
        out_shape=jax.ShapeDtypeStruct((2, nodes_hi, LANES), jnp.float32),
        in_specs=[vmem] * 8 + [pl.BlockSpec(memory_space=pltpu.SMEM)],
        out_specs=vmem,
        scratch_shapes=[
            pltpu.VMEM((2, rows, chunks, LANES), jnp.float32),
            pltpu.VMEM((2, rows, chunks, LANES), jnp.float32),
            pltpu.VMEM((rows, chunks, LANES), jnp.float32),
            pltpu.VMEM((rows, chunks, LANES), jnp.float32),
            pltpu.VMEM((2 * nodes_hi, 2 * LANES), jnp.bfloat16),
            pltpu.VMEM((2, 2 * LANES, 3 * slots), jnp.bfloat16),
            pltpu.VMEM((2, 3, slots), jnp.int32),
            pltpu.VMEM((STEPS, 2, 3, chunks, LANES), jnp.float32),
            pltpu.VMEM((STEPS, 2, 3, chunks, LANES), jnp.float32),
            pltpu.VMEM((STEPS, 2, 3, 2, slots), jnp.float32),
            pltpu.VMEM((STEPS, 2, 3, 2, slots), jnp.float32),
            pltpu.VMEM((2, 3, 1, slots), jnp.float32),
            dma((STEPS, 2)),
            dma((STEPS, 2)),
            dma((STEPS, 2, 3)),
            dma((STEPS, 2, 3)),
            dma((3,)),
            dma((3,)),
        ],
        compiler_params=pltpu.CompilerParams(
            collective_id=0, has_side_effects=True, vmem_limit_bytes=24 * 1024 * 1024
        ),
    )(
        interleaved(displacement), interleaved(stiffness)[0], weight[0], offset[0],
        srow[0], scol[0], trow[0], tcol[0], count,
    )
    out = out.reshape(2, chunks, rows, LANES).transpose(0, 2, 1, 3)
    return out.reshape(1, 2, rows, width)


def solution(mesh):
    placed = (
        P("sec", None, "tile", None),
        P("sec", "tile", None),
        P("sec", "tile", None),
        P("sec", None, "tile", None),
        P("sec", "tile", None),
        P("sec", "tile", None),
        P("sec", "tile", None),
        P("sec", "tile", None),
        P("sec", "tile"),
    )
    return jax.shard_map(
        functools.partial(relax, mesh.shape["sec"], mesh.shape["tile"]),
        mesh=mesh, in_specs=placed, out_specs=P("sec", None, "tile", None), check_vma=False,
    )
```

```python
import functools
import jax
import jax.numpy as jnp
from jax import lax
from jax.experimental import pallas as pl
from jax.experimental.pallas import tpu as pltpu
from jax.sharding import PartitionSpec as P

STEPS = 2
DAMPING = 0.7
LANES = 128
MESH = pl.DeviceIdType.MESH


def stencil(rows, above, below):
    chunks = rows[0].shape[0]
    lane = lax.broadcasted_iota(jnp.int32, rows[0].shape, 1)
    chunk = lax.broadcasted_iota(jnp.int32, rows[0].shape, 0)
    sums = []
    for here, beside in ((rows[0], above + rows[1]), (rows[1], rows[0] + below)):
        both = here + 0.5 * beside
        left = pltpu.roll(both, 1, 1)
        left = jnp.where(lane == 0, jnp.where(chunk == 0, 0.0, pltpu.roll(left, 1, 0)), left)
        right = pltpu.roll(both, LANES - 1, 1)
        right = jnp.where(
            lane == LANES - 1,
            jnp.where(chunk == chunks - 1, 0.0, pltpu.roll(right, chunks - 1, 0)),
            right,
        )
        sums.append(beside + left + right)
    return sums


def two_parts(values):
    high = values.astype(jnp.bfloat16)
    low = (values - high.astype(jnp.float32)).astype(jnp.bfloat16)
    return high, low


def kernel(
    n_sec, n_tile, disp_in, stiff_in, wgt_in, off_in, srow_in, scol_in, trow_in, tcol_in, cnt_in,
    out,
    disp, stiff, wgt, off, rows, cols, cnt, load_sem,
    field, force, total, inv, lhs, hot_lo, hot_hi, hi_ids, edge, halo, mine, theirs, weights,
    edge_send, edge_recv, val_send, val_recv, wgt_send, wgt_recv,
):
    sec = lax.axis_index("sec")
    tile = lax.axis_index("tile")
    chunks = field.shape[2]
    nodes_hi = 2 * chunks
    slots = wgt.shape[2]
    has_tile = [tile > 0, None, tile < n_tile - 1]
    has_sec = [sec < n_sec - 1, sec > 0]
    sec_of = [sec + 1, sec - 1]
    sides = ((0, 0), (2, 1))

    def when_tile(g, body):
        if has_tile[g] is None:
            body()
        else:
            pl.when(has_tile[g])(body)

    barrier = pltpu.get_barrier_semaphore()

    def greet(s, t):
        pl.semaphore_signal(barrier, inc=1, device_id=(s, t), device_id_type=MESH)

    for g in (0, 2):
        when_tile(g, lambda g=g: greet(sec, tile + g - 1))
    for role in range(2):

        @pl.when(has_sec[role])
        def _(role=role):
            for g in (0, 2, 1):
                when_tile(g, lambda g=g: greet(sec_of[role], tile + g - 1))

    low_side = jnp.where(tile > 0, 1, 0)
    high_side = jnp.where(tile < n_tile - 1, 1, 0)
    secs = jnp.where(sec > 0, 1, 0) + jnp.where(sec < n_sec - 1, 1, 0)
    greetings = low_side + high_side + secs * (1 + low_side + high_side)

    loads = [
        pltpu.make_async_copy(source, target, load_sem.at[i])
        for i, (source, target) in enumerate(
            (
                (disp_in, disp),
                (stiff_in, stiff),
                (scol_in, cols.at[0]),
                (srow_in, rows.at[0]),
                (tcol_in, cols.at[1]),
                (trow_in, rows.at[1]),
                (off_in, off),
                (wgt_in, wgt),
                (cnt_in, cnt),
            )
        )
    ]
    for load in loads:
        load.start()

    def edge_copy(step, side, k, landed=False):
        to_side = side if landed else 1 - side
        return pltpu.make_async_remote_copy(
            src_ref=edge.at[step, side, k],
            dst_ref=halo.at[step, to_side, k],
            send_sem=edge_send.at[step, side, k],
            recv_sem=edge_recv.at[step, to_side, k],
            device_id=(sec, tile + 2 * side - 1),
            device_id_type=MESH,
        )

    def value_copy(step, role, g, landed=False):
        to_role, to_g = (role, g) if landed else (1 - role, 2 - g)
        return pltpu.make_async_remote_copy(
            src_ref=mine.at[step, role, g],
            dst_ref=theirs.at[step, to_role, to_g],
            send_sem=val_send.at[step, role, g],
            recv_sem=val_recv.at[step, to_role, to_g],
            device_id=(sec_of[role], tile + g - 1),
            device_id_type=MESH,
        )

    def weight_copy(g, landed=False):
        role = 1 if landed else 0
        to_g = g if landed else 2 - g
        return pltpu.make_async_remote_copy(
            src_ref=weights.at[0, g],
            dst_ref=weights.at[1, to_g],
            send_sem=wgt_send.at[g],
            recv_sem=wgt_recv.at[to_g],
            device_id=(sec_of[role], tile + g - 1),
            device_id_type=MESH,
        )

    def send_edges(step, k):
        for g, side in sides:
            pl.when(has_tile[g])(lambda side=side: edge_copy(step, side, k).start())

    def await_edges(step, k):
        for g, side in sides:
            pl.when(has_tile[g])(lambda side=side: edge_copy(step, side, k, True).wait_recv())

    for g, side in sides:

        @pl.when(jnp.logical_not(has_tile[g]))
        def _(g=g, side=side):
            halo[:, side] = jnp.zeros((STEPS,) + halo.shape[2:], jnp.float32)
            for role in range(2):
                weights[role, g] = jnp.zeros(weights.shape[2:], jnp.float32)
                for step in range(STEPS):
                    theirs[step, role, g] = jnp.zeros(theirs.shape[3:], jnp.float32)

    lane_slot = lax.broadcasted_iota(jnp.int32, (1, slots), 1)
    lo_node = lax.broadcasted_iota(jnp.int32, (LANES, slots), 0)
    hi_node = lax.broadcasted_iota(jnp.int32, (nodes_hi, slots), 0)

    loads[0].wait()
    loads[1].wait()
    for r in range(2):
        c_row = stiff[pl.ds(r, chunks, stride=2), :]
        edge[0, r, 2] = c_row
        for k in range(2):
            u_row = disp[k, pl.ds(r, chunks, stride=2), :]
            field[k, r] = u_row
            edge[0, r, k] = c_row * u_row

    for load in loads[2:]:
        load.wait()

    @pl.when(has_sec[0])
    def _():
        for g in range(3):

            def mask(g=g):
                weights[0, g] = jnp.where(lane_slot < cnt[:, g : g + 1], wgt[g], 0.0)

            when_tile(g, mask)

    for role in range(2):

        @pl.when(has_sec[role])
        def _(role=role):
            for g in range(3):
                col = cols[role, g]
                hi = rows[role, g] * chunks + (col >> 7)
                hi_ids[role, g] = hi
                at = pl.ds(g * slots, slots)
                hot = jnp.where(lo_node == (col & (LANES - 1)), 1.0, 0.0).astype(jnp.bfloat16)
                hot_lo[role, pl.ds(0, LANES), at] = hot
                hot_lo[role, pl.ds(LANES, LANES), at] = hot
                hot_hi[role, :, at] = jnp.where(hi_node == hi, 1.0, 0.0).astype(jnp.bfloat16)

    def pick(step, role):
        for g in (0, 2, 1):
            found = jnp.dot(
                lhs[...],
                hot_lo[role, :, pl.ds(g * slots, slots)],
                preferred_element_type=jnp.float32,
            )
            hit = hi_node == hi_ids[role, g]
            for k in range(2):
                value = jnp.sum(
                    jnp.where(hit, found[k * nodes_hi : (k + 1) * nodes_hi], 0.0),
                    axis=0,
                    keepdims=True,
                )
                if role == 0:
                    value = value - off[g, pl.ds(k, 1), :]
                mine[step, role, g, pl.ds(k, 1), :] = value
            when_tile(g, lambda g=g: value_copy(step, role, g).start())

    def spread(role, g, values):
        at = pl.ds(g * slots, slots)
        high = [row.astype(jnp.bfloat16) for row in values]
        low = [(row - h.astype(jnp.float32)).astype(jnp.bfloat16) for row, h in zip(values, high)]
        summed = lax.dot_general(
            jnp.concatenate([hot_hi[role, :, at] * part for part in high + low], axis=0),
            hot_lo[role, pl.ds(0, LANES), at],
            (((1,), (1,)), ((), ())),
            preferred_element_type=jnp.float32,
        )
        half = len(values) * nodes_hi
        return summed[:half] + summed[half:]

    for step in range(STEPS):
        for k in range(2):
            part = two_parts(field[k].reshape(nodes_hi, LANES))
            lhs[pl.ds(k * nodes_hi, nodes_hi), pl.ds(0, LANES)] = part[0]
            lhs[pl.ds(k * nodes_hi, nodes_hi), pl.ds(LANES, LANES)] = part[1]
        if step == 0:
            pl.semaphore_wait(barrier, greetings)
            send_edges(0, 0)

            @pl.when(has_sec[0])
            def _():
                for g in (0, 2, 1):
                    when_tile(g, lambda g=g: weight_copy(g).start())

        for role in range(2):
            pl.when(has_sec[role])(lambda role=role: pick(step, role))

        if step == 0:
            send_edges(0, 2)
        send_edges(step, 1)

        if step == 0:
            inv[...] = jnp.zeros(inv.shape, jnp.float32)
            for role in range(2):

                @pl.when(has_sec[role])
                def _(role=role):
                    for g in range(3):
                        if role == 1:
                            when_tile(g, lambda g=g: weight_copy(g, True).wait_recv())
                        at = spread(role, g, [weights[role, g]])
                        inv[...] += at.reshape(inv.shape)

        force[...] = jnp.zeros(force.shape, jnp.float32)
        for role in range(2):

            @pl.when(has_sec[role])
            def _(role=role):
                for g in (1, 0, 2):
                    when_tile(g, lambda g=g: value_copy(step, role, g, True).wait_recv())
                    pull = weights[role, g] * (theirs[step, role, g] - mine[step, role, g])
                    at = spread(role, g, [pull[0:1], pull[1:2]])
                    force[...] += at.reshape(force.shape)

        if step == 0:
            await_edges(0, 2)
            c_rows = [edge[0, r, 2] for r in range(2)]
            sums = stencil(c_rows, halo[0, 0, 2], halo[0, 1, 2])
            for r in range(2):
                springs = c_rows[r] * sums[r]
                total[r] = springs
                inv[r] = DAMPING / (inv[r] + springs)

        for k in range(2):
            await_edges(step, k)
            sums = stencil([edge[step, r, k] for r in range(2)], halo[step, 0, k], halo[step, 1, k])
            for r in range(2):
                c_row = edge[0, r, 2]
                here = field[k, r]
                pulled = force[k, r] + c_row * sums[r] - here * total[r]
                new = here + pulled * inv[r]
                if step < STEPS - 1:
                    field[k, r] = new
                    edge[step + 1, r, k] = c_row * new
                else:
                    out[k, pl.ds(r, chunks, stride=2), :] = new
            if step < STEPS - 1 and k == 0:
                send_edges(step + 1, 0)

    for step in range(STEPS):
        for k in range(3 if step == 0 else 2):
            for g, side in sides:
                pl.when(has_tile[g])(
                    lambda side=side: edge_copy(step, side, k).wait_send()
                )
        for role in range(2):

            @pl.when(has_sec[role])
            def _(role=role):
                for g in range(3):
                    when_tile(g, lambda g=g: value_copy(step, role, g).wait_send())
                    if step == 0 and role == 0:
                        when_tile(g, lambda g=g: weight_copy(g).wait_send())


def relax(n_sec, n_tile, *args):
    displacement, stiffness, weight, offset, srow, scol, trow, tcol, count = args
    rows, width = stiffness.shape[1:]
    slots = weight.shape[2]
    chunks = width // LANES
    nodes_hi = rows * chunks

    def interleaved(x):
        x = x.reshape(-1, rows, chunks, LANES).transpose(0, 2, 1, 3)
        return x.reshape(-1, nodes_hi, LANES)

    vmem = pl.BlockSpec(memory_space=pltpu.VMEM)
    dma = pltpu.SemaphoreType.DMA
    f32 = jnp.float32
    out = pl.pallas_call(
        functools.partial(kernel, n_sec, n_tile),
        out_shape=jax.ShapeDtypeStruct((2, nodes_hi, LANES), f32),
        in_specs=[pl.BlockSpec(memory_space=pltpu.HBM)] * 9,
        out_specs=vmem,
        scratch_shapes=[
            pltpu.VMEM((2, nodes_hi, LANES), f32),
            pltpu.VMEM((nodes_hi, LANES), f32),
            pltpu.VMEM((3, 1, slots), f32),
            pltpu.VMEM((3, 2, slots), f32),
            pltpu.VMEM((2, 3, 1, slots), jnp.int32),
            pltpu.VMEM((2, 3, 1, slots), jnp.int32),
            pltpu.VMEM((1, 3), jnp.int32),
            dma((9,)),
            pltpu.VMEM((2, rows, chunks, LANES), f32),
            pltpu.VMEM((2, rows, chunks, LANES), f32),
            pltpu.VMEM((rows, chunks, LANES), f32),
            pltpu.VMEM((rows, chunks, LANES), f32),
            pltpu.VMEM((2 * nodes_hi, 2 * LANES), jnp.bfloat16),
            pltpu.VMEM((2, 2 * LANES, 3 * slots), jnp.bfloat16),
            pltpu.VMEM((2, nodes_hi, 3 * slots), jnp.bfloat16),
            pltpu.VMEM((2, 3, 1, slots), jnp.int32),
            pltpu.VMEM((STEPS, 2, 3, chunks, LANES), f32),
            pltpu.VMEM((STEPS, 2, 3, chunks, LANES), f32),
            pltpu.VMEM((STEPS, 2, 3, 2, slots), f32),
            pltpu.VMEM((STEPS, 2, 3, 2, slots), f32),
            pltpu.VMEM((2, 3, 1, slots), f32),
            dma((STEPS, 2, 3)),
            dma((STEPS, 2, 3)),
            dma((STEPS, 2, 3)),
            dma((STEPS, 2, 3)),
            dma((3,)),
            dma((3,)),
        ],
        compiler_params=pltpu.CompilerParams(
            collective_id=0, has_side_effects=True, vmem_limit_bytes=64 * 1024 * 1024
        ),
    )(
        interleaved(displacement), interleaved(stiffness)[0], weight.transpose(1, 0, 2),
        offset[0].transpose(1, 0, 2), srow.transpose(1, 0, 2), scol.transpose(1, 0, 2),
        trow.transpose(1, 0, 2), tcol.transpose(1, 0, 2), count,
    )
    out = out.reshape(2, chunks, rows, LANES).transpose(0, 2, 1, 3)
    return out.reshape(1, 2, rows, width)


def solution(mesh):
    placed = (
        P("sec", None, "tile", None),
        P("sec", "tile", None),
        P("sec", "tile", None),
        P("sec", None, "tile", None),
        P("sec", "tile", None),
        P("sec", "tile", None),
        P("sec", "tile", None),
        P("sec", "tile", None),
        P("sec", "tile"),
    )
    return jax.shard_map(
        functools.partial(relax, mesh.shape["sec"], mesh.shape["tile"]),
        mesh=mesh, in_specs=placed, out_specs=P("sec", None, "tile", None), check_vma=False,
    )
```

```python
import functools
import jax
import jax.numpy as jnp
from jax import lax
from jax.experimental import pallas as pl
from jax.experimental.pallas import tpu as pltpu
from jax.sharding import PartitionSpec as P

STEPS = 2
DAMPING = 0.7
LANES = 128
MESH = pl.DeviceIdType.MESH


def stencil(rows, above, below):
    chunks = rows[0].shape[0]
    lane = lax.broadcasted_iota(jnp.int32, rows[0].shape, 1)
    chunk = lax.broadcasted_iota(jnp.int32, rows[0].shape, 0)
    sums = []
    for here, beside in ((rows[0], above + rows[1]), (rows[1], rows[0] + below)):
        both = here + 0.5 * beside
        left = pltpu.roll(both, 1, 1)
        left = jnp.where(lane == 0, jnp.where(chunk == 0, 0.0, pltpu.roll(left, 1, 0)), left)
        right = pltpu.roll(both, LANES - 1, 1)
        right = jnp.where(
            lane == LANES - 1,
            jnp.where(chunk == chunks - 1, 0.0, pltpu.roll(right, chunks - 1, 0)),
            right,
        )
        sums.append(beside + left + right)
    return sums


def two_parts(values):
    high = values.astype(jnp.bfloat16)
    low = (values - high.astype(jnp.float32)).astype(jnp.bfloat16)
    return high, low


def kernel(
    n_sec, n_tile, disp_in, stiff_in, wgt_in, off_in, srow_in, scol_in, trow_in, tcol_in, cnt_in,
    out,
    disp, stiff, wgt, off, rows, cols, cnt, load_sem,
    field, force, total, inv, lhs, hot_lo, hot_hi, hi_ids, edge, halo, mine, theirs, weights,
    edge_send, edge_recv, val_send, val_recv, wgt_send, wgt_recv,
):
    sec = lax.axis_index("sec")
    tile = lax.axis_index("tile")
    chunks = field.shape[2]
    nodes_hi = 2 * chunks
    slots = wgt.shape[2]
    has_tile = [tile > 0, None, tile < n_tile - 1]
    has_sec = [sec < n_sec - 1, sec > 0]
    sec_of = [sec + 1, sec - 1]
    sides = ((0, 0), (2, 1))

    def when_tile(g, body):
        if has_tile[g] is None:
            body()
        else:
            pl.when(has_tile[g])(body)

    barrier = pltpu.get_barrier_semaphore()

    def greet(s, t):
        pl.semaphore_signal(barrier, inc=1, device_id=(s, t), device_id_type=MESH)

    for g in (0, 2):
        when_tile(g, lambda g=g: greet(sec, tile + g - 1))
    for role in range(2):

        @pl.when(has_sec[role])
        def _(role=role):
            for g in (0, 2, 1):
                when_tile(g, lambda g=g: greet(sec_of[role], tile + g - 1))

    low_side = jnp.where(tile > 0, 1, 0)
    high_side = jnp.where(tile < n_tile - 1, 1, 0)
    secs = jnp.where(sec > 0, 1, 0) + jnp.where(sec < n_sec - 1, 1, 0)
    greetings = low_side + high_side + secs * (1 + low_side + high_side)

    loads = [
        pltpu.make_async_copy(source, target, load_sem.at[i])
        for i, (source, target) in enumerate(
            (
                (disp_in, disp),
                (stiff_in, stiff),
                (scol_in, cols.at[0]),
                (srow_in, rows.at[0]),
                (tcol_in, cols.at[1]),
                (trow_in, rows.at[1]),
                (off_in, off),
                (wgt_in, wgt),
                (cnt_in, cnt),
            )
        )
    ]
    for load in loads:
        load.start()

    def edge_copy(step, side, k, landed=False):
        to_side = side if landed else 1 - side
        return pltpu.make_async_remote_copy(
            src_ref=edge.at[step, side, k],
            dst_ref=halo.at[step, to_side, k],
            send_sem=edge_send.at[step, side, k],
            recv_sem=edge_recv.at[step, to_side, k],
            device_id=(sec, tile + 2 * side - 1),
            device_id_type=MESH,
        )

    def value_copy(step, role, g, landed=False):
        to_role, to_g = (role, g) if landed else (1 - role, 2 - g)
        return pltpu.make_async_remote_copy(
            src_ref=mine.at[step, role, g],
            dst_ref=theirs.at[step, to_role, to_g],
            send_sem=val_send.at[step, role, g],
            recv_sem=val_recv.at[step, to_role, to_g],
            device_id=(sec_of[role], tile + g - 1),
            device_id_type=MESH,
        )

    def weight_copy(g, landed=False):
        role = 1 if landed else 0
        to_g = g if landed else 2 - g
        return pltpu.make_async_remote_copy(
            src_ref=weights.at[0, g],
            dst_ref=weights.at[1, to_g],
            send_sem=wgt_send.at[g],
            recv_sem=wgt_recv.at[to_g],
            device_id=(sec_of[role], tile + g - 1),
            device_id_type=MESH,
        )

    def send_edges(step, k):
        for g, side in sides:
            pl.when(has_tile[g])(lambda side=side: edge_copy(step, side, k).start())

    def await_edges(step, k):
        for g, side in sides:
            pl.when(has_tile[g])(lambda side=side: edge_copy(step, side, k, True).wait_recv())

    for g, side in sides:

        @pl.when(jnp.logical_not(has_tile[g]))
        def _(g=g, side=side):
            halo[:, side] = jnp.zeros((STEPS,) + halo.shape[2:], jnp.float32)
            for role in range(2):
                weights[role, g] = jnp.zeros(weights.shape[2:], jnp.float32)
                for step in range(STEPS):
                    theirs[step, role, g] = jnp.zeros(theirs.shape[3:], jnp.float32)

    lane_slot = lax.broadcasted_iota(jnp.int32, (1, slots), 1)
    lo_node = lax.broadcasted_iota(jnp.int32, (LANES, slots), 0)
    hi_node = lax.broadcasted_iota(jnp.int32, (nodes_hi, slots), 0)

    loads[0].wait()
    loads[1].wait()
    for r in range(2):
        c_row = stiff[pl.ds(r, chunks, stride=2), :]
        edge[0, r, 2] = c_row
        for k in range(2):
            u_row = disp[k, pl.ds(r, chunks, stride=2), :]
            field[k, r] = u_row
            edge[0, r, k] = c_row * u_row

    for load in loads[2:]:
        load.wait()

    @pl.when(has_sec[0])
    def _():
        for g in range(3):

            def mask(g=g):
                weights[0, g] = jnp.where(lane_slot < cnt[:, g : g + 1], wgt[g], 0.0)

            when_tile(g, mask)

    for role in range(2):

        @pl.when(has_sec[role])
        def _(role=role):
            for g in range(3):
                col = cols[role, g]
                hi = rows[role, g] * chunks + (col >> 7)
                hi_ids[role, g] = hi
                at = pl.ds(g * slots, slots)
                hot = jnp.where(lo_node == (col & (LANES - 1)), 1.0, 0.0).astype(jnp.bfloat16)
                hot_lo[role, pl.ds(0, LANES), at] = hot
                hot_lo[role, pl.ds(LANES, LANES), at] = hot
                hot_hi[role, :, at] = jnp.where(hi_node == hi, 1.0, 0.0).astype(jnp.bfloat16)

    def pick(step, role):
        for g in (0, 2, 1):
            found = jnp.dot(
                lhs[...],
                hot_lo[role, :, pl.ds(g * slots, slots)],
                preferred_element_type=jnp.float32,
            )
            hit = hi_node == hi_ids[role, g]
            for k in range(2):
                value = jnp.sum(
                    jnp.where(hit, found[k * nodes_hi : (k + 1) * nodes_hi], 0.0),
                    axis=0,
                    keepdims=True,
                )
                if role == 0:
                    value = value - off[g, pl.ds(k, 1), :]
                mine[step, role, g, pl.ds(k, 1), :] = value
            when_tile(g, lambda g=g: value_copy(step, role, g).start())

    def spread(role, g, values):
        at = pl.ds(g * slots, slots)
        high = [row.astype(jnp.bfloat16) for row in values]
        low = [(row - h.astype(jnp.float32)).astype(jnp.bfloat16) for row, h in zip(values, high)]
        summed = lax.dot_general(
            jnp.concatenate([hot_hi[role, :, at] * part for part in high + low], axis=0),
            hot_lo[role, pl.ds(0, LANES), at],
            (((1,), (1,)), ((), ())),
            preferred_element_type=jnp.float32,
        )
        half = len(values) * nodes_hi
        return summed[:half] + summed[half:]

    for step in range(STEPS):
        for k in range(2):
            part = two_parts(field[k].reshape(nodes_hi, LANES))
            lhs[pl.ds(k * nodes_hi, nodes_hi), pl.ds(0, LANES)] = part[0]
            lhs[pl.ds(k * nodes_hi, nodes_hi), pl.ds(LANES, LANES)] = part[1]
        if step == 0:
            pl.semaphore_wait(barrier, greetings)
            send_edges(0, 0)

            @pl.when(has_sec[0])
            def _():
                for g in (0, 2, 1):
                    when_tile(g, lambda g=g: weight_copy(g).start())

        for role in range(2):
            pl.when(has_sec[role])(lambda role=role: pick(step, role))

        if step == 0:
            send_edges(0, 2)
        send_edges(step, 1)

        if step == 0:
            inv[...] = jnp.zeros(inv.shape, jnp.float32)
            for role in range(2):

                @pl.when(has_sec[role])
                def _(role=role):
                    for g in range(3):
                        if role == 1:
                            when_tile(g, lambda g=g: weight_copy(g, True).wait_recv())
                        at = spread(role, g, [weights[role, g]])
                        inv[...] += at.reshape(inv.shape)

        force[...] = jnp.zeros(force.shape, jnp.float32)
        for role in range(2):

            @pl.when(has_sec[role])
            def _(role=role):
                for g in (1, 0, 2):
                    when_tile(g, lambda g=g: value_copy(step, role, g, True).wait_recv())
                    pull = weights[role, g] * (theirs[step, role, g] - mine[step, role, g])
                    at = spread(role, g, [pull[0:1], pull[1:2]])
                    force[...] += at.reshape(force.shape)

        if step == 0:
            await_edges(0, 2)
            c_rows = [edge[0, r, 2] for r in range(2)]
            sums = stencil(c_rows, halo[0, 0, 2], halo[0, 1, 2])
            for r in range(2):
                springs = c_rows[r] * sums[r]
                total[r] = springs
                inv[r] = DAMPING / (inv[r] + springs)

        for k in range(2):
            await_edges(step, k)
            sums = stencil([edge[step, r, k] for r in range(2)], halo[step, 0, k], halo[step, 1, k])
            for r in range(2):
                c_row = edge[0, r, 2]
                here = field[k, r]
                pulled = force[k, r] + c_row * sums[r] - here * total[r]
                new = here + pulled * inv[r]
                if step < STEPS - 1:
                    field[k, r] = new
                    edge[step + 1, r, k] = c_row * new
                else:
                    out[k, pl.ds(r, chunks, stride=2), :] = new
            if step < STEPS - 1 and k == 0:
                send_edges(step + 1, 0)

    for step in range(STEPS):
        for k in range(3 if step == 0 else 2):
            for g, side in sides:
                pl.when(has_tile[g])(
                    lambda side=side: edge_copy(step, side, k).wait_send()
                )
        for role in range(2):

            @pl.when(has_sec[role])
            def _(role=role):
                for g in range(3):
                    when_tile(g, lambda g=g: value_copy(step, role, g).wait_send())
                    if step == 0 and role == 0:
                        when_tile(g, lambda g=g: weight_copy(g).wait_send())


def relax(n_sec, n_tile, *args):
    displacement, stiffness, weight, offset, srow, scol, trow, tcol, count = args
    rows, width = stiffness.shape[1:]
    slots = weight.shape[2]
    chunks = width // LANES
    nodes_hi = rows * chunks

    def interleaved(x):
        x = x.reshape(-1, rows, chunks, LANES).transpose(0, 2, 1, 3)
        return x.reshape(-1, nodes_hi, LANES)

    operands = (
        interleaved(displacement), interleaved(stiffness)[0], weight.transpose(1, 0, 2),
        offset[0].transpose(1, 0, 2), srow.transpose(1, 0, 2), scol.transpose(1, 0, 2),
        trow.transpose(1, 0, 2), tcol.transpose(1, 0, 2), count,
    )
    vmem = pl.BlockSpec(memory_space=pltpu.VMEM)
    dma = pltpu.SemaphoreType.DMA
    f32 = jnp.float32
    out = pl.pallas_call(
        functools.partial(kernel, n_sec, n_tile),
        out_shape=jax.ShapeDtypeStruct((2, nodes_hi, LANES), f32),
        in_specs=[pl.BlockSpec(memory_space=pltpu.HBM)] * 9,
        out_specs=vmem,
        scratch_shapes=[
            pltpu.VMEM((2, nodes_hi, LANES), f32),
            pltpu.VMEM((nodes_hi, LANES), f32),
            pltpu.VMEM((3, 1, slots), f32),
            pltpu.VMEM((3, 2, slots), f32),
            pltpu.VMEM((2, 3, 1, slots), jnp.int32),
            pltpu.VMEM((2, 3, 1, slots), jnp.int32),
            pltpu.VMEM((1, 3), jnp.int32),
            dma((9,)),
            pltpu.VMEM((2, rows, chunks, LANES), f32),
            pltpu.VMEM((2, rows, chunks, LANES), f32),
            pltpu.VMEM((rows, chunks, LANES), f32),
            pltpu.VMEM((rows, chunks, LANES), f32),
            pltpu.VMEM((2 * nodes_hi, 2 * LANES), jnp.bfloat16),
            pltpu.VMEM((2, 2 * LANES, 3 * slots), jnp.bfloat16),
            pltpu.VMEM((2, nodes_hi, 3 * slots), jnp.bfloat16),
            pltpu.VMEM((2, 3, 1, slots), jnp.int32),
            pltpu.VMEM((STEPS, 2, 3, chunks, LANES), f32),
            pltpu.VMEM((STEPS, 2, 3, chunks, LANES), f32),
            pltpu.VMEM((STEPS, 2, 3, 2, slots), f32),
            pltpu.VMEM((STEPS, 2, 3, 2, slots), f32),
            pltpu.VMEM((2, 3, 1, slots), f32),
            dma((STEPS, 2, 3)),
            dma((STEPS, 2, 3)),
            dma((STEPS, 2, 3)),
            dma((STEPS, 2, 3)),
            dma((3,)),
            dma((3,)),
        ],
        compiler_params=pltpu.CompilerParams(
            collective_id=0, has_side_effects=True, vmem_limit_bytes=24 * 1024 * 1024
        ),
    )(*[pltpu.with_memory_space_constraint(x, pltpu.HBM) for x in operands])
    out = out.reshape(2, chunks, rows, LANES).transpose(0, 2, 1, 3)
    return out.reshape(1, 2, rows, width)


def solution(mesh):
    placed = (
        P("sec", None, "tile", None),
        P("sec", "tile", None),
        P("sec", "tile", None),
        P("sec", None, "tile", None),
        P("sec", "tile", None),
        P("sec", "tile", None),
        P("sec", "tile", None),
        P("sec", "tile", None),
        P("sec", "tile"),
    )
    return jax.shard_map(
        functools.partial(relax, mesh.shape["sec"], mesh.shape["tile"]),
        mesh=mesh, in_specs=placed, out_specs=P("sec", None, "tile", None), check_vma=False,
    )
```

```python
import functools
import jax
import jax.numpy as jnp
from jax import lax
from jax.experimental import pallas as pl
from jax.experimental.pallas import tpu as pltpu
from jax.sharding import PartitionSpec as P

STEPS = 2
DAMPING = 0.7
LANES = 128
MESH = pl.DeviceIdType.MESH


def stencil(rows, above, below):
    chunks = rows[0].shape[0]
    lane = lax.broadcasted_iota(jnp.int32, rows[0].shape, 1)
    chunk = lax.broadcasted_iota(jnp.int32, rows[0].shape, 0)
    sums = []
    for here, beside in ((rows[0], above + rows[1]), (rows[1], rows[0] + below)):
        both = here + 0.5 * beside
        left = pltpu.roll(both, 1, 1)
        left = jnp.where(lane == 0, jnp.where(chunk == 0, 0.0, pltpu.roll(left, 1, 0)), left)
        right = pltpu.roll(both, LANES - 1, 1)
        right = jnp.where(
            lane == LANES - 1,
            jnp.where(chunk == chunks - 1, 0.0, pltpu.roll(right, chunks - 1, 0)),
            right,
        )
        sums.append(beside + left + right)
    return sums


def two_parts(values):
    high = values.astype(jnp.bfloat16)
    low = (values - high.astype(jnp.float32)).astype(jnp.bfloat16)
    return high, low


def kernel(
    n_sec, n_tile, disp_in, stiff_in, wgt_in, off_in, srow_in, scol_in, trow_in, tcol_in, cnt_in,
    out,
    disp, stiff, wgt, off, rows, cols, cnt, load_sem,
    field, force, total, inv, lhs, hot_lo, hot_hi, hi_ids, edge, halo, mine, theirs, weights,
    edge_send, edge_recv, val_send, val_recv, wgt_send, wgt_recv,
):
    sec = lax.axis_index("sec")
    tile = lax.axis_index("tile")
    chunks = field.shape[2]
    nodes_hi = 2 * chunks
    slots = wgt.shape[2]
    has_tile = [tile > 0, None, tile < n_tile - 1]
    first_role = jnp.where(sec < n_sec - 1, 0, 1)
    end_role = jnp.where(sec > 0, 2, 1)
    sides = ((0, 0), (2, 1))

    def when_tile(g, body):
        if has_tile[g] is None:
            body()
        else:
            pl.when(has_tile[g])(body)

    def each_role(body):
        def turn(role, carry):
            body(role)
            return carry

        lax.fori_loop(first_role, end_role, turn, jnp.int32(0))

    barrier = pltpu.get_barrier_semaphore()

    def greet(s, t):
        pl.semaphore_signal(barrier, inc=1, device_id=(s, t), device_id_type=MESH)

    for g in (0, 2):
        when_tile(g, lambda g=g: greet(sec, tile + g - 1))
    def greet_role(role):
        for g in (0, 2, 1):
            when_tile(g, lambda g=g: greet(sec + 1 - 2 * role, tile + g - 1))

    each_role(greet_role)

    low_side = jnp.where(tile > 0, 1, 0)
    high_side = jnp.where(tile < n_tile - 1, 1, 0)
    secs = jnp.where(sec > 0, 1, 0) + jnp.where(sec < n_sec - 1, 1, 0)
    greetings = low_side + high_side + secs * (1 + low_side + high_side)

    loads = [
        pltpu.make_async_copy(source, target, load_sem.at[i])
        for i, (source, target) in enumerate(
            (
                (disp_in, disp),
                (stiff_in, stiff),
                (scol_in, cols.at[0]),
                (srow_in, rows.at[0]),
                (tcol_in, cols.at[1]),
                (trow_in, rows.at[1]),
                (off_in, off.at[0]),
                (wgt_in, wgt),
                (cnt_in, cnt),
            )
        )
    ]
    for load in loads:
        load.start()

    def edge_copy(step, side, k, landed=False):
        to_side = side if landed else 1 - side
        return pltpu.make_async_remote_copy(
            src_ref=edge.at[step, side, k],
            dst_ref=halo.at[step, to_side, k],
            send_sem=edge_send.at[step, side, k],
            recv_sem=edge_recv.at[step, to_side, k],
            device_id=(sec, tile + 2 * side - 1),
            device_id_type=MESH,
        )

    def value_copy(step, role, g, landed=False):
        to_role, to_g = (role, g) if landed else (1 - role, 2 - g)
        return pltpu.make_async_remote_copy(
            src_ref=mine.at[step, role, g],
            dst_ref=theirs.at[step, to_role, to_g],
            send_sem=val_send.at[step, role, g],
            recv_sem=val_recv.at[step, to_role, to_g],
            device_id=(sec + 1 - 2 * role, tile + g - 1),
            device_id_type=MESH,
        )

    def weight_copy(g, landed=False):
        role = 1 if landed else 0
        to_g = g if landed else 2 - g
        return pltpu.make_async_remote_copy(
            src_ref=weights.at[0, g],
            dst_ref=weights.at[1, to_g],
            send_sem=wgt_send.at[g],
            recv_sem=wgt_recv.at[to_g],
            device_id=(sec + 1 - 2 * role, tile + g - 1),
            device_id_type=MESH,
        )

    def send_edges(step, k):
        for g, side in sides:
            pl.when(has_tile[g])(lambda side=side: edge_copy(step, side, k).start())

    def await_edges(step, k):
        for g, side in sides:
            pl.when(has_tile[g])(lambda side=side: edge_copy(step, side, k, True).wait_recv())

    for g, side in sides:

        @pl.when(jnp.logical_not(has_tile[g]))
        def _(g=g, side=side):
            halo[:, side] = jnp.zeros((STEPS,) + halo.shape[2:], jnp.float32)
            for role in range(2):
                weights[role, g] = jnp.zeros(weights.shape[2:], jnp.float32)
                for step in range(STEPS):
                    theirs[step, role, g] = jnp.zeros(theirs.shape[3:], jnp.float32)

    lane_slot = lax.broadcasted_iota(jnp.int32, (1, slots), 1)
    lo_node = lax.broadcasted_iota(jnp.int32, (LANES, slots), 0)
    hi_node = lax.broadcasted_iota(jnp.int32, (nodes_hi, slots), 0)

    loads[0].wait()
    loads[1].wait()
    for r in range(2):
        c_row = stiff[pl.ds(r, chunks, stride=2), :]
        edge[0, r, 2] = c_row
        for k in range(2):
            u_row = disp[k, pl.ds(r, chunks, stride=2), :]
            field[k, r] = u_row
            edge[0, r, k] = c_row * u_row

    for load in loads[2:]:
        load.wait()

    off[1] = jnp.zeros(off.shape[1:], jnp.float32)

    @pl.when(sec < n_sec - 1)
    def _():
        for g in range(3):

            def mask(g=g):
                weights[0, g] = jnp.where(lane_slot < cnt[:, g : g + 1], wgt[g], 0.0)

            when_tile(g, mask)

    def prepare(role):
        for g in range(3):
            col = cols[role, g]
            hi = rows[role, g] * chunks + (col >> 7)
            hi_ids[role, g] = hi
            at = pl.ds(g * slots, slots)
            hot = jnp.where(lo_node == (col & (LANES - 1)), 1.0, 0.0).astype(jnp.bfloat16)
            hot_lo[role, pl.ds(0, LANES), at] = hot
            hot_lo[role, pl.ds(LANES, LANES), at] = hot
            hot_hi[role, :, at] = jnp.where(hi_node == hi, 1.0, 0.0).astype(jnp.bfloat16)

    each_role(prepare)

    def pick(step, role):
        for g in (0, 2, 1):
            found = jnp.dot(
                lhs[...],
                hot_lo[role, :, pl.ds(g * slots, slots)],
                preferred_element_type=jnp.float32,
            )
            hit = hi_node == hi_ids[role, g]
            for k in range(2):
                value = jnp.sum(
                    jnp.where(hit, found[k * nodes_hi : (k + 1) * nodes_hi], 0.0),
                    axis=0,
                    keepdims=True,
                )
                mine[step, role, g, pl.ds(k, 1), :] = value - off[role, g, pl.ds(k, 1), :]
        for g in (0, 2, 1):
            when_tile(g, lambda g=g: value_copy(step, role, g).start())

    def spread(role, g, values):
        at = pl.ds(g * slots, slots)
        high = [row.astype(jnp.bfloat16) for row in values]
        low = [(row - h.astype(jnp.float32)).astype(jnp.bfloat16) for row, h in zip(values, high)]
        summed = lax.dot_general(
            jnp.concatenate([hot_hi[role, :, at] * part for part in high + low], axis=0),
            hot_lo[role, pl.ds(0, LANES), at],
            (((1,), (1,)), ((), ())),
            preferred_element_type=jnp.float32,
        )
        half = len(values) * nodes_hi
        return summed[:half] + summed[half:]

    for step in range(STEPS):
        for k in range(2):
            part = two_parts(field[k].reshape(nodes_hi, LANES))
            lhs[pl.ds(k * nodes_hi, nodes_hi), pl.ds(0, LANES)] = part[0]
            lhs[pl.ds(k * nodes_hi, nodes_hi), pl.ds(LANES, LANES)] = part[1]
        if step == 0:
            pl.semaphore_wait(barrier, greetings)
            send_edges(0, 0)

            @pl.when(sec < n_sec - 1)
            def _():
                for g in (0, 2, 1):
                    when_tile(g, lambda g=g: weight_copy(g).start())

        each_role(functools.partial(pick, step))

        if step == 0:
            send_edges(0, 2)
        send_edges(step, 1)

        if step == 0:
            inv[...] = jnp.zeros(inv.shape, jnp.float32)

            def spread_weights(role):
                @pl.when(role == 1)
                def _():
                    for g in range(3):
                        when_tile(g, lambda g=g: weight_copy(g, True).wait_recv())

                at = sum(spread(role, g, [weights[role, g]]) for g in range(3))
                inv[...] += at.reshape(inv.shape)

            each_role(spread_weights)

        force[...] = jnp.zeros(force.shape, jnp.float32)

        def spread_pulls(role, step=step):
            for batch in ((1,), (0, 2)):
                for g in batch:
                    when_tile(g, lambda g=g: value_copy(step, role, g, True).wait_recv())
                at = 0.0
                for g in batch:
                    pull = weights[role, g] * (theirs[step, role, g] - mine[step, role, g])
                    at = at + spread(role, g, [pull[0:1], pull[1:2]])
                force[...] += at.reshape(force.shape)

        each_role(spread_pulls)

        if step == 0:
            await_edges(0, 2)
            c_rows = [edge[0, r, 2] for r in range(2)]
            sums = stencil(c_rows, halo[0, 0, 2], halo[0, 1, 2])
            for r in range(2):
                springs = c_rows[r] * sums[r]
                total[r] = springs
                inv[r] = DAMPING / (inv[r] + springs)

        for k in range(2):
            await_edges(step, k)
            sums = stencil([edge[step, r, k] for r in range(2)], halo[step, 0, k], halo[step, 1, k])
            for r in range(2):
                c_row = edge[0, r, 2]
                here = field[k, r]
                pulled = force[k, r] + c_row * sums[r] - here * total[r]
                new = here + pulled * inv[r]
                if step < STEPS - 1:
                    field[k, r] = new
                    edge[step + 1, r, k] = c_row * new
                else:
                    out[k, pl.ds(r, chunks, stride=2), :] = new
            if step < STEPS - 1 and k == 0:
                send_edges(step + 1, 0)

    for step in range(STEPS):
        for k in range(3 if step == 0 else 2):
            for g, side in sides:
                pl.when(has_tile[g])(
                    lambda side=side: edge_copy(step, side, k).wait_send()
                )

        def drain(role, step=step):
            for g in range(3):
                when_tile(g, lambda g=g: value_copy(step, role, g).wait_send())

        each_role(drain)

    @pl.when(sec < n_sec - 1)
    def _():
        for g in range(3):
            when_tile(g, lambda g=g: weight_copy(g).wait_send())


def relax(n_sec, n_tile, *args):
    displacement, stiffness, weight, offset, srow, scol, trow, tcol, count = args
    rows, width = stiffness.shape[1:]
    slots = weight.shape[2]
    chunks = width // LANES
    nodes_hi = rows * chunks

    def interleaved(x):
        x = x.reshape(-1, rows, chunks, LANES).transpose(0, 2, 1, 3)
        return x.reshape(-1, nodes_hi, LANES)

    operands = (
        interleaved(displacement), interleaved(stiffness)[0], weight.transpose(1, 0, 2),
        offset[0].transpose(1, 0, 2), srow.transpose(1, 0, 2), scol.transpose(1, 0, 2),
        trow.transpose(1, 0, 2), tcol.transpose(1, 0, 2), count,
    )
    vmem = pl.BlockSpec(memory_space=pltpu.VMEM)
    dma = pltpu.SemaphoreType.DMA
    f32 = jnp.float32
    out = pl.pallas_call(
        functools.partial(kernel, n_sec, n_tile),
        out_shape=jax.ShapeDtypeStruct((2, nodes_hi, LANES), f32),
        in_specs=[pl.BlockSpec(memory_space=pltpu.HBM)] * 9,
        out_specs=vmem,
        scratch_shapes=[
            pltpu.VMEM((2, nodes_hi, LANES), f32),
            pltpu.VMEM((nodes_hi, LANES), f32),
            pltpu.VMEM((3, 1, slots), f32),
            pltpu.VMEM((2, 3, 2, slots), f32),
            pltpu.VMEM((2, 3, 1, slots), jnp.int32),
            pltpu.VMEM((2, 3, 1, slots), jnp.int32),
            pltpu.VMEM((1, 3), jnp.int32),
            dma((9,)),
            pltpu.VMEM((2, rows, chunks, LANES), f32),
            pltpu.VMEM((2, rows, chunks, LANES), f32),
            pltpu.VMEM((rows, chunks, LANES), f32),
            pltpu.VMEM((rows, chunks, LANES), f32),
            pltpu.VMEM((2 * nodes_hi, 2 * LANES), jnp.bfloat16),
            pltpu.VMEM((2, 2 * LANES, 3 * slots), jnp.bfloat16),
            pltpu.VMEM((2, nodes_hi, 3 * slots), jnp.bfloat16),
            pltpu.VMEM((2, 3, 1, slots), jnp.int32),
            pltpu.VMEM((STEPS, 2, 3, chunks, LANES), f32),
            pltpu.VMEM((STEPS, 2, 3, chunks, LANES), f32),
            pltpu.VMEM((STEPS, 2, 3, 2, slots), f32),
            pltpu.VMEM((STEPS, 2, 3, 2, slots), f32),
            pltpu.VMEM((2, 3, 1, slots), f32),
            dma((STEPS, 2, 3)),
            dma((STEPS, 2, 3)),
            dma((STEPS, 2, 3)),
            dma((STEPS, 2, 3)),
            dma((3,)),
            dma((3,)),
        ],
        compiler_params=pltpu.CompilerParams(
            collective_id=0, has_side_effects=True, vmem_limit_bytes=24 * 1024 * 1024
        ),
    )(*[pltpu.with_memory_space_constraint(x, pltpu.HBM) for x in operands])
    out = out.reshape(2, chunks, rows, LANES).transpose(0, 2, 1, 3)
    return out.reshape(1, 2, rows, width)


def solution(mesh):
    placed = (
        P("sec", None, "tile", None),
        P("sec", "tile", None),
        P("sec", "tile", None),
        P("sec", None, "tile", None),
        P("sec", "tile", None),
        P("sec", "tile", None),
        P("sec", "tile", None),
        P("sec", "tile", None),
        P("sec", "tile"),
    )
    return jax.shard_map(
        functools.partial(relax, mesh.shape["sec"], mesh.shape["tile"]),
        mesh=mesh, in_specs=placed, out_specs=P("sec", None, "tile", None), check_vma=False,
    )
```

```python
import functools
import jax
import jax.numpy as jnp
from jax import lax
from jax.experimental import pallas as pl
from jax.experimental.pallas import tpu as pltpu
from jax.sharding import PartitionSpec as P

STEPS = 2
DAMPING = 0.7
LANES = 128
MESH = pl.DeviceIdType.MESH


def stencil(rows, above, below):
    chunks = rows[0].shape[0]
    lane = lax.broadcasted_iota(jnp.int32, rows[0].shape, 1)
    chunk = lax.broadcasted_iota(jnp.int32, rows[0].shape, 0)
    sums = []
    for here, beside in ((rows[0], above + rows[1]), (rows[1], rows[0] + below)):
        both = here + 0.5 * beside
        left = pltpu.roll(both, 1, 1)
        left = jnp.where(lane == 0, jnp.where(chunk == 0, 0.0, pltpu.roll(left, 1, 0)), left)
        right = pltpu.roll(both, LANES - 1, 1)
        right = jnp.where(
            lane == LANES - 1,
            jnp.where(chunk == chunks - 1, 0.0, pltpu.roll(right, chunks - 1, 0)),
            right,
        )
        sums.append(beside + left + right)
    return sums


def two_parts(values):
    high = values.astype(jnp.bfloat16)
    low = (values - high.astype(jnp.float32)).astype(jnp.bfloat16)
    return high, low


def kernel(
    n_sec, n_tile, disp_in, stiff_in, wgt_in, off_in, srow_in, scol_in, trow_in, tcol_in, cnt_in,
    out,
    disp, stiff, wgt, off, rows, cols, cnt, load_sem,
    field, force, total, inv, lhs, hot_lo, hot_hi, hi_ids, edge, halo, mine, theirs, weights,
    edge_send, edge_recv, val_send, val_recv, wgt_send, wgt_recv,
):
    sec = lax.axis_index("sec")
    tile = lax.axis_index("tile")
    chunks = field.shape[2]
    nodes_hi = 2 * chunks
    slots = wgt.shape[2]
    has_tile = [tile > 0, None, tile < n_tile - 1]
    first_role = jnp.where(sec < n_sec - 1, 0, 1)
    end_role = jnp.where(sec > 0, 2, 1)
    sides = ((0, 0), (2, 1))

    def when_tile(g, body):
        if has_tile[g] is None:
            body()
        else:
            pl.when(has_tile[g])(body)

    def each_role(body):
        def turn(role, carry):
            body(role)
            return carry

        lax.fori_loop(first_role, end_role, turn, jnp.int32(0))

    barrier = pltpu.get_barrier_semaphore()

    def greet(s, t):
        pl.semaphore_signal(barrier, inc=1, device_id=(s, t), device_id_type=MESH)

    for g in (0, 2):
        when_tile(g, lambda g=g: greet(sec, tile + g - 1))
    def greet_role(role):
        for g in (0, 2, 1):
            when_tile(g, lambda g=g: greet(sec + 1 - 2 * role, tile + g - 1))

    each_role(greet_role)

    low_side = jnp.where(tile > 0, 1, 0)
    high_side = jnp.where(tile < n_tile - 1, 1, 0)
    secs = jnp.where(sec > 0, 1, 0) + jnp.where(sec < n_sec - 1, 1, 0)
    greetings = low_side + high_side + secs * (1 + low_side + high_side)

    loads = [
        pltpu.make_async_copy(source, target, load_sem.at[i])
        for i, (source, target) in enumerate(
            (
                (disp_in, disp),
                (stiff_in, stiff),
                (scol_in, cols.at[0]),
                (srow_in, rows.at[0]),
                (tcol_in, cols.at[1]),
                (trow_in, rows.at[1]),
                (off_in, off.at[0]),
                (wgt_in, wgt),
                (cnt_in, cnt),
            )
        )
    ]
    for load in loads:
        load.start()

    def edge_copy(step, side, k, landed=False):
        to_side = side if landed else 1 - side
        return pltpu.make_async_remote_copy(
            src_ref=edge.at[step, side, k],
            dst_ref=halo.at[step, to_side, k],
            send_sem=edge_send.at[step, side, k],
            recv_sem=edge_recv.at[step, to_side, k],
            device_id=(sec, tile + 2 * side - 1),
            device_id_type=MESH,
        )

    def value_copy(step, role, g, landed=False):
        to_role, to_g = (role, g) if landed else (1 - role, 2 - g)
        return pltpu.make_async_remote_copy(
            src_ref=mine.at[step, role, g],
            dst_ref=theirs.at[step, to_role, to_g],
            send_sem=val_send.at[step, role, g],
            recv_sem=val_recv.at[step, to_role, to_g],
            device_id=(sec + 1 - 2 * role, tile + g - 1),
            device_id_type=MESH,
        )

    def weight_copy(g, landed=False):
        role = 1 if landed else 0
        to_g = g if landed else 2 - g
        return pltpu.make_async_remote_copy(
            src_ref=weights.at[0, g],
            dst_ref=weights.at[1, to_g],
            send_sem=wgt_send.at[g],
            recv_sem=wgt_recv.at[to_g],
            device_id=(sec + 1 - 2 * role, tile + g - 1),
            device_id_type=MESH,
        )

    def send_edges(step, k):
        for g, side in sides:
            pl.when(has_tile[g])(lambda side=side: edge_copy(step, side, k).start())

    def await_edges(step, k):
        for g, side in sides:
            pl.when(has_tile[g])(lambda side=side: edge_copy(step, side, k, True).wait_recv())

    for g, side in sides:

        @pl.when(jnp.logical_not(has_tile[g]))
        def _(g=g, side=side):
            halo[:, side] = jnp.zeros((STEPS,) + halo.shape[2:], jnp.float32)
            for role in range(2):
                weights[role, g] = jnp.zeros(weights.shape[2:], jnp.float32)
                for step in range(STEPS):
                    theirs[step, role, g] = jnp.zeros(theirs.shape[3:], jnp.float32)

    lane_slot = lax.broadcasted_iota(jnp.int32, (1, slots), 1)
    lo_node = lax.broadcasted_iota(jnp.int32, (LANES, slots), 0)
    hi_node = lax.broadcasted_iota(jnp.int32, (nodes_hi, slots), 0)

    loads[0].wait()
    loads[1].wait()
    for r in range(2):
        c_row = stiff[pl.ds(r, chunks, stride=2), :]
        edge[0, r, 2] = c_row
        for k in range(2):
            u_row = disp[k, pl.ds(r, chunks, stride=2), :]
            field[k, r] = u_row
            edge[0, r, k] = c_row * u_row

    pl.semaphore_wait(barrier, greetings)
    send_edges(0, 0)
    send_edges(0, 2)
    for load in loads[2:]:
        load.wait()

    off[1] = jnp.zeros(off.shape[1:], jnp.float32)

    @pl.when(sec < n_sec - 1)
    def _():
        for g in range(3):

            def mask(g=g):
                weights[0, g] = jnp.where(lane_slot < cnt[:, g : g + 1], wgt[g], 0.0)

            when_tile(g, mask)

    def prepare(role):
        for g in range(3):
            col = cols[role, g]
            hi = rows[role, g] * chunks + (col >> 7)
            hi_ids[role, g] = hi
            at = pl.ds(g * slots, slots)
            hot = jnp.where(lo_node == (col & (LANES - 1)), 1.0, 0.0).astype(jnp.bfloat16)
            hot_lo[role, pl.ds(0, LANES), at] = hot
            hot_lo[role, pl.ds(LANES, LANES), at] = hot
            hot_hi[role, :, at] = jnp.where(hi_node == hi, 1.0, 0.0).astype(jnp.bfloat16)

    each_role(prepare)

    def pick(step, role):
        for g in (0, 2, 1):
            found = jnp.dot(
                lhs[...],
                hot_lo[role, :, pl.ds(g * slots, slots)],
                preferred_element_type=jnp.float32,
            )
            hit = hi_node == hi_ids[role, g]
            for k in range(2):
                value = jnp.sum(
                    jnp.where(hit, found[k * nodes_hi : (k + 1) * nodes_hi], 0.0),
                    axis=0,
                    keepdims=True,
                )
                mine[step, role, g, pl.ds(k, 1), :] = value - off[role, g, pl.ds(k, 1), :]
        for g in (0, 2, 1):
            when_tile(g, lambda g=g: value_copy(step, role, g).start())

    def spread(role, g, values):
        at = pl.ds(g * slots, slots)
        high = [row.astype(jnp.bfloat16) for row in values]
        low = [(row - h.astype(jnp.float32)).astype(jnp.bfloat16) for row, h in zip(values, high)]
        summed = lax.dot_general(
            jnp.concatenate([hot_hi[role, :, at] * part for part in high + low], axis=0),
            hot_lo[role, pl.ds(0, LANES), at],
            (((1,), (1,)), ((), ())),
            preferred_element_type=jnp.float32,
        )
        half = len(values) * nodes_hi
        return summed[:half] + summed[half:]

    def drain(step):
        def drain_role(role):
            for g in range(3):
                when_tile(g, lambda g=g: value_copy(step, role, g).wait_send())

        each_role(drain_role)
        if step == 0:

            @pl.when(sec < n_sec - 1)
            def _():
                for g in range(3):
                    when_tile(g, lambda g=g: weight_copy(g).wait_send())

        for g, side in sides:

            @pl.when(has_tile[g])
            def _(side=side):
                for k in range(3 if step == 0 else 2):
                    edge_copy(step, side, k).wait_send()

    for step in range(STEPS):
        for k in range(2):
            part = two_parts(field[k].reshape(nodes_hi, LANES))
            lhs[pl.ds(k * nodes_hi, nodes_hi), pl.ds(0, LANES)] = part[0]
            lhs[pl.ds(k * nodes_hi, nodes_hi), pl.ds(LANES, LANES)] = part[1]
        if step == 0:

            @pl.when(sec < n_sec - 1)
            def _():
                for g in (0, 2, 1):
                    when_tile(g, lambda g=g: weight_copy(g).start())

        each_role(functools.partial(pick, step))

        send_edges(step, 1)
        if step > 0:
            drain(step - 1)

        if step == 0:
            inv[...] = jnp.zeros(inv.shape, jnp.float32)

            def spread_weights(role):
                @pl.when(role == 1)
                def _():
                    for g in range(3):
                        when_tile(g, lambda g=g: weight_copy(g, True).wait_recv())

                at = sum(spread(role, g, [weights[role, g]]) for g in range(3))
                inv[...] += at.reshape(inv.shape)

            each_role(spread_weights)

        force[...] = jnp.zeros(force.shape, jnp.float32)

        def spread_pulls(role, step=step):
            for batch in ((1,), (0, 2)):
                for g in batch:
                    when_tile(g, lambda g=g: value_copy(step, role, g, True).wait_recv())
                at = 0.0
                for g in batch:
                    pull = weights[role, g] * (theirs[step, role, g] - mine[step, role, g])
                    at = at + spread(role, g, [pull[0:1], pull[1:2]])
                force[...] += at.reshape(force.shape)

        each_role(spread_pulls)

        if step == 0:
            await_edges(0, 2)
            c_rows = [edge[0, r, 2] for r in range(2)]
            sums = stencil(c_rows, halo[0, 0, 2], halo[0, 1, 2])
            for r in range(2):
                springs = c_rows[r] * sums[r]
                total[r] = springs
                inv[r] = DAMPING / (inv[r] + springs)

        for k in range(2):
            await_edges(step, k)
            sums = stencil([edge[step, r, k] for r in range(2)], halo[step, 0, k], halo[step, 1, k])
            for r in range(2):
                c_row = edge[0, r, 2]
                here = field[k, r]
                pulled = force[k, r] + c_row * sums[r] - here * total[r]
                new = here + pulled * inv[r]
                if step < STEPS - 1:
                    field[k, r] = new
                    edge[step + 1, r, k] = c_row * new
                else:
                    out[k, pl.ds(r, chunks, stride=2), :] = new
            if step < STEPS - 1 and k == 0:
                send_edges(step + 1, 0)

    drain(STEPS - 1)


def relax(n_sec, n_tile, *args):
    displacement, stiffness, weight, offset, srow, scol, trow, tcol, count = args
    rows, width = stiffness.shape[1:]
    slots = weight.shape[2]
    chunks = width // LANES
    nodes_hi = rows * chunks

    def interleaved(x):
        x = x.reshape(-1, rows, chunks, LANES).transpose(0, 2, 1, 3)
        return x.reshape(-1, nodes_hi, LANES)

    operands = (
        interleaved(displacement), interleaved(stiffness)[0], weight.transpose(1, 0, 2),
        offset[0].transpose(1, 0, 2), srow.transpose(1, 0, 2), scol.transpose(1, 0, 2),
        trow.transpose(1, 0, 2), tcol.transpose(1, 0, 2), count,
    )
    vmem = pl.BlockSpec(memory_space=pltpu.VMEM)
    dma = pltpu.SemaphoreType.DMA
    f32 = jnp.float32
    out = pl.pallas_call(
        functools.partial(kernel, n_sec, n_tile),
        out_shape=jax.ShapeDtypeStruct((2, nodes_hi, LANES), f32),
        in_specs=[pl.BlockSpec(memory_space=pltpu.HBM)] * 9,
        out_specs=vmem,
        scratch_shapes=[
            pltpu.VMEM((2, nodes_hi, LANES), f32),
            pltpu.VMEM((nodes_hi, LANES), f32),
            pltpu.VMEM((3, 1, slots), f32),
            pltpu.VMEM((2, 3, 2, slots), f32),
            pltpu.VMEM((2, 3, 1, slots), jnp.int32),
            pltpu.VMEM((2, 3, 1, slots), jnp.int32),
            pltpu.VMEM((1, 3), jnp.int32),
            dma((9,)),
            pltpu.VMEM((2, rows, chunks, LANES), f32),
            pltpu.VMEM((2, rows, chunks, LANES), f32),
            pltpu.VMEM((rows, chunks, LANES), f32),
            pltpu.VMEM((rows, chunks, LANES), f32),
            pltpu.VMEM((2 * nodes_hi, 2 * LANES), jnp.bfloat16),
            pltpu.VMEM((2, 2 * LANES, 3 * slots), jnp.bfloat16),
            pltpu.VMEM((2, nodes_hi, 3 * slots), jnp.bfloat16),
            pltpu.VMEM((2, 3, 1, slots), jnp.int32),
            pltpu.VMEM((STEPS, 2, 3, chunks, LANES), f32),
            pltpu.VMEM((STEPS, 2, 3, chunks, LANES), f32),
            pltpu.VMEM((STEPS, 2, 3, 2, slots), f32),
            pltpu.VMEM((STEPS, 2, 3, 2, slots), f32),
            pltpu.VMEM((2, 3, 1, slots), f32),
            dma((STEPS, 2, 3)),
            dma((STEPS, 2, 3)),
            dma((STEPS, 2, 3)),
            dma((STEPS, 2, 3)),
            dma((3,)),
            dma((3,)),
        ],
        compiler_params=pltpu.CompilerParams(
            collective_id=0, has_side_effects=True, vmem_limit_bytes=24 * 1024 * 1024
        ),
    )(*[pltpu.with_memory_space_constraint(x, pltpu.HBM) for x in operands])
    out = out.reshape(2, chunks, rows, LANES).transpose(0, 2, 1, 3)
    return out.reshape(1, 2, rows, width)


def solution(mesh):
    placed = (
        P("sec", None, "tile", None),
        P("sec", "tile", None),
        P("sec", "tile", None),
        P("sec", None, "tile", None),
        P("sec", "tile", None),
        P("sec", "tile", None),
        P("sec", "tile", None),
        P("sec", "tile", None),
        P("sec", "tile"),
    )
    return jax.shard_map(
        functools.partial(relax, mesh.shape["sec"], mesh.shape["tile"]),
        mesh=mesh, in_specs=placed, out_specs=P("sec", None, "tile", None), check_vma=False,
    )
```

```python
import functools
import jax
import jax.numpy as jnp
from jax import lax
from jax.experimental import pallas as pl
from jax.experimental.pallas import tpu as pltpu
from jax.sharding import PartitionSpec as P

STEPS = 2
DAMPING = 0.7
LANES = 128
MESH = pl.DeviceIdType.MESH


def stencil(rows, above, below):
    chunks = rows[0].shape[0]
    lane = lax.broadcasted_iota(jnp.int32, rows[0].shape, 1)
    chunk = lax.broadcasted_iota(jnp.int32, rows[0].shape, 0)
    sums = []
    for here, beside in ((rows[0], above + rows[1]), (rows[1], rows[0] + below)):
        both = here + 0.5 * beside
        left = pltpu.roll(both, 1, 1)
        left = jnp.where(lane == 0, jnp.where(chunk == 0, 0.0, pltpu.roll(left, 1, 0)), left)
        right = pltpu.roll(both, LANES - 1, 1)
        right = jnp.where(
            lane == LANES - 1,
            jnp.where(chunk == chunks - 1, 0.0, pltpu.roll(right, chunks - 1, 0)),
            right,
        )
        sums.append(beside + left + right)
    return sums


def two_parts(values):
    high = values.astype(jnp.bfloat16)
    low = (values - high.astype(jnp.float32)).astype(jnp.bfloat16)
    return high, low


def kernel(
    n_sec, n_tile, disp_in, stiff_in, wgt_in, off_in, srow_in, scol_in, trow_in, tcol_in, cnt_in,
    out,
    disp, stiff, wgt, off, rows, cols, cnt, load_sem,
    field, force, total, inv, lhs, hot_lo, hot_hi, hi_ids, edge, halo, mine, theirs, weights,
    edge_send, edge_recv, val_send, val_recv, wgt_send, wgt_recv,
):
    sec = lax.axis_index("sec")
    tile = lax.axis_index("tile")
    chunks = field.shape[2]
    nodes_hi = 2 * chunks
    slots = wgt.shape[2]
    has_tile = [tile > 0, None, tile < n_tile - 1]
    first_role = jnp.where(sec < n_sec - 1, 0, 1)
    end_role = jnp.where(sec > 0, 2, 1)
    sides = ((0, 0), (2, 1))

    def when_tile(g, body):
        if has_tile[g] is None:
            body()
        else:
            pl.when(has_tile[g])(body)

    def each_role(body):
        def turn(role, carry):
            body(role)
            return carry

        lax.fori_loop(first_role, end_role, turn, jnp.int32(0))

    barrier = pltpu.get_barrier_semaphore()

    def greet(s, t):
        pl.semaphore_signal(barrier, inc=1, device_id=(s, t), device_id_type=MESH)

    for g in (0, 2):
        when_tile(g, lambda g=g: greet(sec, tile + g - 1))
    def greet_role(role):
        for g in (0, 2, 1):
            when_tile(g, lambda g=g: greet(sec + 1 - 2 * role, tile + g - 1))

    each_role(greet_role)

    low_side = jnp.where(tile > 0, 1, 0)
    high_side = jnp.where(tile < n_tile - 1, 1, 0)
    secs = jnp.where(sec > 0, 1, 0) + jnp.where(sec < n_sec - 1, 1, 0)
    greetings = low_side + high_side + secs * (1 + low_side + high_side)

    loads = [
        pltpu.make_async_copy(source, target, load_sem.at[i])
        for i, (source, target) in enumerate(
            (
                (disp_in, disp),
                (stiff_in, stiff),
                (scol_in, cols.at[0]),
                (srow_in, rows.at[0]),
                (tcol_in, cols.at[1]),
                (trow_in, rows.at[1]),
                (off_in, off.at[0]),
                (wgt_in, wgt),
                (cnt_in, cnt),
            )
        )
    ]
    for load in loads:
        load.start()

    def edge_copy(step, side, k, landed=False):
        to_side = side if landed else 1 - side
        return pltpu.make_async_remote_copy(
            src_ref=edge.at[step, side, k],
            dst_ref=halo.at[step, to_side, k],
            send_sem=edge_send.at[step, side, k],
            recv_sem=edge_recv.at[step, to_side, k],
            device_id=(sec, tile + 2 * side - 1),
            device_id_type=MESH,
        )

    def value_copy(step, role, g, landed=False):
        to_role, to_g = (role, g) if landed else (1 - role, 2 - g)
        return pltpu.make_async_remote_copy(
            src_ref=mine.at[step, role, g],
            dst_ref=theirs.at[step, to_role, to_g],
            send_sem=val_send.at[step, role, g],
            recv_sem=val_recv.at[step, to_role, to_g],
            device_id=(sec + 1 - 2 * role, tile + g - 1),
            device_id_type=MESH,
        )

    def weight_copy(g, landed=False):
        role = 1 if landed else 0
        to_g = g if landed else 2 - g
        return pltpu.make_async_remote_copy(
            src_ref=weights.at[0, g],
            dst_ref=weights.at[1, to_g],
            send_sem=wgt_send.at[g],
            recv_sem=wgt_recv.at[to_g],
            device_id=(sec + 1 - 2 * role, tile + g - 1),
            device_id_type=MESH,
        )

    def send_edges(step, k):
        for g, side in sides:
            pl.when(has_tile[g])(lambda side=side: edge_copy(step, side, k).start())

    def await_edges(step, k):
        for g, side in sides:
            pl.when(has_tile[g])(lambda side=side: edge_copy(step, side, k, True).wait_recv())

    for g, side in sides:

        @pl.when(jnp.logical_not(has_tile[g]))
        def _(g=g, side=side):
            halo[:, side] = jnp.zeros((STEPS,) + halo.shape[2:], jnp.float32)
            for role in range(2):
                weights[role, g] = jnp.zeros(weights.shape[2:], jnp.float32)
                for step in range(STEPS):
                    theirs[step, role, g] = jnp.zeros(theirs.shape[3:], jnp.float32)

    lane_slot = lax.broadcasted_iota(jnp.int32, (1, slots), 1)
    lo_node = lax.broadcasted_iota(jnp.int32, (LANES, slots), 0)
    hi_node = lax.broadcasted_iota(jnp.int32, (nodes_hi, slots), 0)

    loads[0].wait()
    loads[1].wait()
    for r in range(2):
        c_row = stiff[pl.ds(r, chunks, stride=2), :]
        edge[0, r, 2] = c_row
        for k in range(2):
            u_row = disp[k, pl.ds(r, chunks, stride=2), :]
            field[k, r] = u_row
            edge[0, r, k] = c_row * u_row

    for load in loads[2:]:
        load.wait()

    off[1] = jnp.zeros(off.shape[1:], jnp.float32)

    @pl.when(sec < n_sec - 1)
    def _():
        for g in range(3):

            def mask(g=g):
                weights[0, g] = jnp.where(lane_slot < cnt[:, g : g + 1], wgt[g], 0.0)

            when_tile(g, mask)

    def prepare(role):
        for g in range(3):
            col = cols[role, g]
            hi = rows[role, g] * chunks + (col >> 7)
            hi_ids[role, g] = hi
            at = pl.ds(g * slots, slots)
            hot = jnp.where(lo_node == (col & (LANES - 1)), 1.0, 0.0).astype(jnp.bfloat16)
            hot_lo[role, pl.ds(0, LANES), at] = hot
            hot_lo[role, pl.ds(LANES, LANES), at] = hot
            hot_hi[role, :, at] = jnp.where(hi_node == hi, 1.0, 0.0).astype(jnp.bfloat16)

    each_role(prepare)

    def pick(step, role):
        for g in (0, 2, 1):
            found = jnp.dot(
                lhs[...],
                hot_lo[role, :, pl.ds(g * slots, slots)],
                preferred_element_type=jnp.float32,
            )
            hit = hi_node == hi_ids[role, g]
            for k in range(2):
                value = jnp.sum(
                    jnp.where(hit, found[k * nodes_hi : (k + 1) * nodes_hi], 0.0),
                    axis=0,
                    keepdims=True,
                )
                mine[step, role, g, pl.ds(k, 1), :] = value - off[role, g, pl.ds(k, 1), :]

    def send_values(step, role):
        for g in (0, 2, 1):
            when_tile(g, lambda g=g: value_copy(step, role, g).start())

    def spread(role, g, values):
        at = pl.ds(g * slots, slots)
        high = [row.astype(jnp.bfloat16) for row in values]
        low = [(row - h.astype(jnp.float32)).astype(jnp.bfloat16) for row, h in zip(values, high)]
        summed = lax.dot_general(
            jnp.concatenate([hot_hi[role, :, at] * part for part in high + low], axis=0),
            hot_lo[role, pl.ds(0, LANES), at],
            (((1,), (1,)), ((), ())),
            preferred_element_type=jnp.float32,
        )
        half = len(values) * nodes_hi
        return summed[:half] + summed[half:]

    def drain(step):
        def drain_role(role):
            for g in range(3):
                when_tile(g, lambda g=g: value_copy(step, role, g).wait_send())

        each_role(drain_role)
        if step == 0:

            @pl.when(sec < n_sec - 1)
            def _():
                for g in range(3):
                    when_tile(g, lambda g=g: weight_copy(g).wait_send())

        for g, side in sides:

            @pl.when(has_tile[g])
            def _(side=side):
                for k in range(3 if step == 0 else 2):
                    edge_copy(step, side, k).wait_send()

    for step in range(STEPS):
        for k in range(2):
            part = two_parts(field[k].reshape(nodes_hi, LANES))
            lhs[pl.ds(k * nodes_hi, nodes_hi), pl.ds(0, LANES)] = part[0]
            lhs[pl.ds(k * nodes_hi, nodes_hi), pl.ds(LANES, LANES)] = part[1]
        each_role(functools.partial(pick, step))
        if step == 0:
            pl.semaphore_wait(barrier, greetings)
        each_role(functools.partial(send_values, step))
        if step == 0:

            @pl.when(sec < n_sec - 1)
            def _():
                for g in (0, 2, 1):
                    when_tile(g, lambda g=g: weight_copy(g).start())

            send_edges(0, 0)
            send_edges(0, 2)
        send_edges(step, 1)
        if step > 0:
            drain(step - 1)

        if step == 0:
            inv[...] = jnp.zeros(inv.shape, jnp.float32)

            def spread_weights(role):
                @pl.when(role == 1)
                def _():
                    for g in range(3):
                        when_tile(g, lambda g=g: weight_copy(g, True).wait_recv())

                at = sum(spread(role, g, [weights[role, g]]) for g in range(3))
                inv[...] += at.reshape(inv.shape)

            each_role(spread_weights)

        force[...] = jnp.zeros(force.shape, jnp.float32)

        def spread_pulls(role, step=step):
            for batch in ((1,), (0, 2)):
                for g in batch:
                    when_tile(g, lambda g=g: value_copy(step, role, g, True).wait_recv())
                at = 0.0
                for g in batch:
                    pull = weights[role, g] * (theirs[step, role, g] - mine[step, role, g])
                    at = at + spread(role, g, [pull[0:1], pull[1:2]])
                force[...] += at.reshape(force.shape)

        each_role(spread_pulls)

        if step == 0:
            await_edges(0, 2)
            c_rows = [edge[0, r, 2] for r in range(2)]
            sums = stencil(c_rows, halo[0, 0, 2], halo[0, 1, 2])
            for r in range(2):
                springs = c_rows[r] * sums[r]
                total[r] = springs
                inv[r] = DAMPING / (inv[r] + springs)

        for k in range(2):
            await_edges(step, k)
            sums = stencil([edge[step, r, k] for r in range(2)], halo[step, 0, k], halo[step, 1, k])
            for r in range(2):
                c_row = edge[0, r, 2]
                here = field[k, r]
                pulled = force[k, r] + c_row * sums[r] - here * total[r]
                new = here + pulled * inv[r]
                if step < STEPS - 1:
                    field[k, r] = new
                    edge[step + 1, r, k] = c_row * new
                else:
                    out[k, pl.ds(r, chunks, stride=2), :] = new
            if step < STEPS - 1 and k == 0:
                send_edges(step + 1, 0)

    drain(STEPS - 1)


def relax(n_sec, n_tile, *args):
    displacement, stiffness, weight, offset, srow, scol, trow, tcol, count = args
    rows, width = stiffness.shape[1:]
    slots = weight.shape[2]
    chunks = width // LANES
    nodes_hi = rows * chunks

    def interleaved(x):
        x = x.reshape(-1, rows, chunks, LANES).transpose(0, 2, 1, 3)
        return x.reshape(-1, nodes_hi, LANES)

    operands = (
        interleaved(displacement), interleaved(stiffness)[0], weight.transpose(1, 0, 2),
        offset[0].transpose(1, 0, 2), srow.transpose(1, 0, 2), scol.transpose(1, 0, 2),
        trow.transpose(1, 0, 2), tcol.transpose(1, 0, 2), count,
    )
    vmem = pl.BlockSpec(memory_space=pltpu.VMEM)
    dma = pltpu.SemaphoreType.DMA
    f32 = jnp.float32
    out = pl.pallas_call(
        functools.partial(kernel, n_sec, n_tile),
        out_shape=jax.ShapeDtypeStruct((2, nodes_hi, LANES), f32),
        in_specs=[pl.BlockSpec(memory_space=pltpu.HBM)] * 9,
        out_specs=vmem,
        scratch_shapes=[
            pltpu.VMEM((2, nodes_hi, LANES), f32),
            pltpu.VMEM((nodes_hi, LANES), f32),
            pltpu.VMEM((3, 1, slots), f32),
            pltpu.VMEM((2, 3, 2, slots), f32),
            pltpu.VMEM((2, 3, 1, slots), jnp.int32),
            pltpu.VMEM((2, 3, 1, slots), jnp.int32),
            pltpu.VMEM((1, 3), jnp.int32),
            dma((9,)),
            pltpu.VMEM((2, rows, chunks, LANES), f32),
            pltpu.VMEM((2, rows, chunks, LANES), f32),
            pltpu.VMEM((rows, chunks, LANES), f32),
            pltpu.VMEM((rows, chunks, LANES), f32),
            pltpu.VMEM((2 * nodes_hi, 2 * LANES), jnp.bfloat16),
            pltpu.VMEM((2, 2 * LANES, 3 * slots), jnp.bfloat16),
            pltpu.VMEM((2, nodes_hi, 3 * slots), jnp.bfloat16),
            pltpu.VMEM((2, 3, 1, slots), jnp.int32),
            pltpu.VMEM((STEPS, 2, 3, chunks, LANES), f32),
            pltpu.VMEM((STEPS, 2, 3, chunks, LANES), f32),
            pltpu.VMEM((STEPS, 2, 3, 2, slots), f32),
            pltpu.VMEM((STEPS, 2, 3, 2, slots), f32),
            pltpu.VMEM((2, 3, 1, slots), f32),
            dma((STEPS, 2, 3)),
            dma((STEPS, 2, 3)),
            dma((STEPS, 2, 3)),
            dma((STEPS, 2, 3)),
            dma((3,)),
            dma((3,)),
        ],
        compiler_params=pltpu.CompilerParams(
            collective_id=0, has_side_effects=True, vmem_limit_bytes=24 * 1024 * 1024
        ),
    )(*[pltpu.with_memory_space_constraint(x, pltpu.HBM) for x in operands])
    out = out.reshape(2, chunks, rows, LANES).transpose(0, 2, 1, 3)
    return out.reshape(1, 2, rows, width)


def solution(mesh):
    placed = (
        P("sec", None, "tile", None),
        P("sec", "tile", None),
        P("sec", "tile", None),
        P("sec", None, "tile", None),
        P("sec", "tile", None),
        P("sec", "tile", None),
        P("sec", "tile", None),
        P("sec", "tile", None),
        P("sec", "tile"),
    )
    return jax.shard_map(
        functools.partial(relax, mesh.shape["sec"], mesh.shape["tile"]),
        mesh=mesh, in_specs=placed, out_specs=P("sec", None, "tile", None), check_vma=False,
    )
```

```python
import functools
import jax
import jax.numpy as jnp
from jax import lax
from jax.experimental import pallas as pl
from jax.experimental.pallas import tpu as pltpu
from jax.sharding import PartitionSpec as P

STEPS = 2
DAMPING = 0.7
LANES = 128
MESH = pl.DeviceIdType.MESH


def stencil(rows, above, below):
    chunks = rows[0].shape[0]
    lane = lax.broadcasted_iota(jnp.int32, rows[0].shape, 1)
    chunk = lax.broadcasted_iota(jnp.int32, rows[0].shape, 0)
    sums = []
    for here, beside in ((rows[0], above + rows[1]), (rows[1], rows[0] + below)):
        both = here + 0.5 * beside
        left = pltpu.roll(both, 1, 1)
        left = jnp.where(lane == 0, jnp.where(chunk == 0, 0.0, pltpu.roll(left, 1, 0)), left)
        right = pltpu.roll(both, LANES - 1, 1)
        right = jnp.where(
            lane == LANES - 1,
            jnp.where(chunk == chunks - 1, 0.0, pltpu.roll(right, chunks - 1, 0)),
            right,
        )
        sums.append(beside + left + right)
    return sums


def two_parts(values):
    high = values.astype(jnp.bfloat16)
    low = (values - high.astype(jnp.float32)).astype(jnp.bfloat16)
    return high, low


def kernel(
    n_sec, n_tile, disp_in, stiff_in, wgt_in, off_in, srow_in, scol_in, trow_in, tcol_in, cnt_in,
    out,
    disp, stiff, wgt, off, rows, cols, cnt, load_sem,
    field, force, total, inv, lhs, hot_lo, hot_hi, hi_ids, edge, halo, mine, theirs, weights,
    edge_send, edge_recv, val_send, val_recv, wgt_send, wgt_recv,
):
    sec = lax.axis_index("sec")
    tile = lax.axis_index("tile")
    chunks = field.shape[2]
    nodes_hi = 2 * chunks
    slots = wgt.shape[2]
    has_tile = [tile > 0, None, tile < n_tile - 1]
    first_role = jnp.where(sec < n_sec - 1, 0, 1)
    end_role = jnp.where(sec > 0, 2, 1)
    sides = ((0, 0), (2, 1))

    def when_tile(g, body):
        if has_tile[g] is None:
            body()
        else:
            pl.when(has_tile[g])(body)

    def each_role(body):
        def turn(role, carry):
            body(role)
            return carry

        lax.fori_loop(first_role, end_role, turn, jnp.int32(0))

    low_side = jnp.where(tile > 0, 1, 0)
    high_side = jnp.where(tile < n_tile - 1, 1, 0)

    def each_group(body):
        def turn(g, carry):
            body(g)
            return carry

        lax.fori_loop(1 - low_side, 2 + high_side, turn, jnp.int32(0))

    def each_side(body):
        def turn(side, carry):
            body(side)
            return carry

        lax.fori_loop(1 - low_side, 1 + high_side, turn, jnp.int32(0))

    barrier = pltpu.get_barrier_semaphore()

    def greet(s, t):
        pl.semaphore_signal(barrier, inc=1, device_id=(s, t), device_id_type=MESH)

    each_side(lambda side: greet(sec, tile + 2 * side - 1))
    def greet_role(role):
        each_group(lambda g: greet(sec + 1 - 2 * role, tile + g - 1))

    each_role(greet_role)

    secs = jnp.where(sec > 0, 1, 0) + jnp.where(sec < n_sec - 1, 1, 0)
    greetings = low_side + high_side + secs * (1 + low_side + high_side)

    loads = [
        pltpu.make_async_copy(source, target, load_sem.at[i])
        for i, (source, target) in enumerate(
            (
                (disp_in, disp),
                (stiff_in, stiff),
                (scol_in, cols.at[0]),
                (srow_in, rows.at[0]),
                (tcol_in, cols.at[1]),
                (trow_in, rows.at[1]),
                (off_in, off.at[0]),
                (wgt_in, wgt),
                (cnt_in, cnt),
            )
        )
    ]
    for load in loads:
        load.start()

    def edge_copy(step, side, k, landed=False):
        to_side = side if landed else 1 - side
        return pltpu.make_async_remote_copy(
            src_ref=edge.at[step, side, k],
            dst_ref=halo.at[step, to_side, k],
            send_sem=edge_send.at[step, side, k],
            recv_sem=edge_recv.at[step, to_side, k],
            device_id=(sec, tile + 2 * side - 1),
            device_id_type=MESH,
        )

    def value_copy(step, role, g, landed=False):
        to_role, to_g = (role, g) if landed else (1 - role, 2 - g)
        return pltpu.make_async_remote_copy(
            src_ref=mine.at[step, role, g],
            dst_ref=theirs.at[step, to_role, to_g],
            send_sem=val_send.at[step, role, g],
            recv_sem=val_recv.at[step, to_role, to_g],
            device_id=(sec + 1 - 2 * role, tile + g - 1),
            device_id_type=MESH,
        )

    def weight_copy(g, landed=False):
        role = 1 if landed else 0
        to_g = g if landed else 2 - g
        return pltpu.make_async_remote_copy(
            src_ref=weights.at[0, g],
            dst_ref=weights.at[1, to_g],
            send_sem=wgt_send.at[g],
            recv_sem=wgt_recv.at[to_g],
            device_id=(sec + 1 - 2 * role, tile + g - 1),
            device_id_type=MESH,
        )

    def send_edges(step, k):
        each_side(lambda side: edge_copy(step, side, k).start())

    def await_edges(step, k):
        each_side(lambda side: edge_copy(step, side, k, True).wait_recv())

    for g, side in sides:

        @pl.when(jnp.logical_not(has_tile[g]))
        def _(g=g, side=side):
            halo[:, side] = jnp.zeros((STEPS,) + halo.shape[2:], jnp.float32)
            for role in range(2):
                weights[role, g] = jnp.zeros(weights.shape[2:], jnp.float32)
                for step in range(STEPS):
                    theirs[step, role, g] = jnp.zeros(theirs.shape[3:], jnp.float32)

    lane_slot = lax.broadcasted_iota(jnp.int32, (1, slots), 1)
    lo_node = lax.broadcasted_iota(jnp.int32, (LANES, slots), 0)
    hi_node = lax.broadcasted_iota(jnp.int32, (nodes_hi, slots), 0)

    loads[0].wait()
    loads[1].wait()
    for r in range(2):
        c_row = stiff[pl.ds(r, chunks, stride=2), :]
        edge[0, r, 2] = c_row
        for k in range(2):
            u_row = disp[k, pl.ds(r, chunks, stride=2), :]
            field[k, r] = u_row
            edge[0, r, k] = c_row * u_row

    for load in loads[2:]:
        load.wait()

    off[1] = jnp.zeros(off.shape[1:], jnp.float32)

    @pl.when(sec < n_sec - 1)
    def _():
        for g in range(3):

            def mask(g=g):
                weights[0, g] = jnp.where(lane_slot < cnt[:, g : g + 1], wgt[g], 0.0)

            when_tile(g, mask)

    def prepare(role):
        def one_group(g, carry):
            col = cols[role, g]
            hi = rows[role, g] * chunks + (col >> 7)
            hi_ids[role, g] = hi
            hot = jnp.where(lo_node == (col & (LANES - 1)), 1.0, 0.0).astype(jnp.bfloat16)
            hot_lo[role, g, pl.ds(0, LANES)] = hot
            hot_lo[role, g, pl.ds(LANES, LANES)] = hot
            hot_hi[role, g] = jnp.where(hi_node == hi, 1.0, 0.0).astype(jnp.bfloat16)
            return carry

        lax.fori_loop(0, 3, one_group, jnp.int32(0))

    each_role(prepare)

    def pick(step, role):
        for g in (0, 2, 1):
            found = jnp.dot(
                lhs[...],
                hot_lo[role, g],
                preferred_element_type=jnp.float32,
            )
            hit = hi_node == hi_ids[role, g]
            for k in range(2):
                value = jnp.sum(
                    jnp.where(hit, found[k * nodes_hi : (k + 1) * nodes_hi], 0.0),
                    axis=0,
                    keepdims=True,
                )
                mine[step, role, g, pl.ds(k, 1), :] = value - off[role, g, pl.ds(k, 1), :]

    def send_values(step, role):
        each_group(lambda g: value_copy(step, role, g).start())

    def spread(role, g, values):
        high = [row.astype(jnp.bfloat16) for row in values]
        low = [(row - h.astype(jnp.float32)).astype(jnp.bfloat16) for row, h in zip(values, high)]
        summed = lax.dot_general(
            jnp.concatenate([hot_hi[role, g] * part for part in high + low], axis=0),
            hot_lo[role, g, pl.ds(0, LANES)],
            (((1,), (1,)), ((), ())),
            preferred_element_type=jnp.float32,
        )
        half = len(values) * nodes_hi
        return summed[:half] + summed[half:]

    def drain(step):
        def drain_role(role):
            each_group(lambda g: value_copy(step, role, g).wait_send())

        def drain_side(side):
            for k in range(2):
                edge_copy(step, side, k).wait_send()

        each_role(drain_role)
        each_side(drain_side)

    def spread_weights(role):
        @pl.when(role == 1)
        def _():
            each_group(lambda g: weight_copy(g, True).wait_recv())

        at = sum(spread(role, g, [weights[role, g]]) for g in range(3))
        inv[...] += at.reshape(inv.shape)

    def one_step(step, carry):
        for k in range(2):
            part = two_parts(field[k].reshape(nodes_hi, LANES))
            lhs[pl.ds(k * nodes_hi, nodes_hi), pl.ds(0, LANES)] = part[0]
            lhs[pl.ds(k * nodes_hi, nodes_hi), pl.ds(LANES, LANES)] = part[1]
        each_role(functools.partial(pick, step))

        @pl.when(step == 0)
        def _():
            pl.semaphore_wait(barrier, greetings)

        each_role(functools.partial(send_values, step))

        @pl.when(step == 0)
        def _():
            @pl.when(sec < n_sec - 1)
            def _():
                each_group(lambda g: weight_copy(g).start())

            send_edges(0, 0)
            send_edges(0, 2)

        send_edges(step, 1)

        @pl.when(step == 0)
        def _():
            inv[...] = jnp.zeros(inv.shape, jnp.float32)
            each_role(spread_weights)

        @pl.when(step > 0)
        def _():
            drain(step - 1)

        force[...] = jnp.zeros(force.shape, jnp.float32)

        def spread_pulls(role):
            for batch in ((1,), (0, 2)):
                for g in batch:
                    when_tile(g, lambda g=g: value_copy(step, role, g, True).wait_recv())
                at = 0.0
                for g in batch:
                    pull = weights[role, g] * (theirs[step, role, g] - mine[step, role, g])
                    at = at + spread(role, g, [pull[0:1], pull[1:2]])
                force[...] += at.reshape(force.shape)

        each_role(spread_pulls)

        @pl.when(step == 0)
        def _():
            await_edges(0, 2)
            c_rows = [edge[0, r, 2] for r in range(2)]
            sums = stencil(c_rows, halo[0, 0, 2], halo[0, 1, 2])
            for r in range(2):
                springs = c_rows[r] * sums[r]
                total[r] = springs
                inv[r] = DAMPING / (inv[r] + springs)

        for k in range(2):
            await_edges(step, k)
            sums = stencil([edge[step, r, k] for r in range(2)], halo[step, 0, k], halo[step, 1, k])
            for r in range(2):
                c_row = edge[0, r, 2]
                here = field[k, r]
                pulled = force[k, r] + c_row * sums[r] - here * total[r]
                new = here + pulled * inv[r]
                field[k, r] = new
                edge[step + 1, r, k] = c_row * new
            if k == 0:

                @pl.when(step < STEPS - 1)
                def _():
                    send_edges(step + 1, 0)

        return carry

    lax.fori_loop(0, STEPS, one_step, jnp.int32(0))
    for k in range(2):
        for r in range(2):
            out[k, pl.ds(r, chunks, stride=2), :] = field[k, r]
    drain(STEPS - 1)
    each_side(lambda side: edge_copy(0, side, 2).wait_send())

    @pl.when(sec < n_sec - 1)
    def _():
        each_group(lambda g: weight_copy(g).wait_send())


def relax(n_sec, n_tile, *args):
    displacement, stiffness, weight, offset, srow, scol, trow, tcol, count = args
    rows, width = stiffness.shape[1:]
    slots = weight.shape[2]
    chunks = width // LANES
    nodes_hi = rows * chunks

    def interleaved(x):
        x = x.reshape(-1, rows, chunks, LANES).transpose(0, 2, 1, 3)
        return x.reshape(-1, nodes_hi, LANES)

    operands = (
        interleaved(displacement), interleaved(stiffness)[0], weight.transpose(1, 0, 2),
        offset[0].transpose(1, 0, 2), srow.transpose(1, 0, 2), scol.transpose(1, 0, 2),
        trow.transpose(1, 0, 2), tcol.transpose(1, 0, 2), count,
    )
    vmem = pl.BlockSpec(memory_space=pltpu.VMEM)
    dma = pltpu.SemaphoreType.DMA
    f32 = jnp.float32
    out = pl.pallas_call(
        functools.partial(kernel, n_sec, n_tile),
        out_shape=jax.ShapeDtypeStruct((2, nodes_hi, LANES), f32),
        in_specs=[pl.BlockSpec(memory_space=pltpu.HBM)] * 9,
        out_specs=vmem,
        scratch_shapes=[
            pltpu.VMEM((2, nodes_hi, LANES), f32),
            pltpu.VMEM((nodes_hi, LANES), f32),
            pltpu.VMEM((3, 1, slots), f32),
            pltpu.VMEM((2, 3, 2, slots), f32),
            pltpu.VMEM((2, 3, 1, slots), jnp.int32),
            pltpu.VMEM((2, 3, 1, slots), jnp.int32),
            pltpu.VMEM((1, 3), jnp.int32),
            dma((9,)),
            pltpu.VMEM((2, rows, chunks, LANES), f32),
            pltpu.VMEM((2, rows, chunks, LANES), f32),
            pltpu.VMEM((rows, chunks, LANES), f32),
            pltpu.VMEM((rows, chunks, LANES), f32),
            pltpu.VMEM((2 * nodes_hi, 2 * LANES), jnp.bfloat16),
            pltpu.VMEM((2, 3, 2 * LANES, slots), jnp.bfloat16),
            pltpu.VMEM((2, 3, nodes_hi, slots), jnp.bfloat16),
            pltpu.VMEM((2, 3, 1, slots), jnp.int32),
            pltpu.VMEM((STEPS + 1, 2, 3, chunks, LANES), f32),
            pltpu.VMEM((STEPS, 2, 3, chunks, LANES), f32),
            pltpu.VMEM((STEPS, 2, 3, 2, slots), f32),
            pltpu.VMEM((STEPS, 2, 3, 2, slots), f32),
            pltpu.VMEM((2, 3, 1, slots), f32),
            dma((STEPS, 2, 3)),
            dma((STEPS, 2, 3)),
            dma((STEPS, 2, 3)),
            dma((STEPS, 2, 3)),
            dma((3,)),
            dma((3,)),
        ],
        compiler_params=pltpu.CompilerParams(
            collective_id=0, has_side_effects=True, vmem_limit_bytes=24 * 1024 * 1024
        ),
    )(*[pltpu.with_memory_space_constraint(x, pltpu.HBM) for x in operands])
    out = out.reshape(2, chunks, rows, LANES).transpose(0, 2, 1, 3)
    return out.reshape(1, 2, rows, width)


def solution(mesh):
    placed = (
        P("sec", None, "tile", None),
        P("sec", "tile", None),
        P("sec", "tile", None),
        P("sec", None, "tile", None),
        P("sec", "tile", None),
        P("sec", "tile", None),
        P("sec", "tile", None),
        P("sec", "tile", None),
        P("sec", "tile"),
    )
    return jax.shard_map(
        functools.partial(relax, mesh.shape["sec"], mesh.shape["tile"]),
        mesh=mesh, in_specs=placed, out_specs=P("sec", None, "tile", None), check_vma=False,
    )
```

```python
import functools
import jax
import jax.numpy as jnp
from jax import lax
from jax.experimental import pallas as pl
from jax.experimental.pallas import tpu as pltpu
from jax.sharding import PartitionSpec as P

STEPS = 2
DAMPING = 0.7
LANES = 128
MESH = pl.DeviceIdType.MESH


def stencil(rows, above, below):
    chunks = rows[0].shape[0]
    lane = lax.broadcasted_iota(jnp.int32, rows[0].shape, 1)
    chunk = lax.broadcasted_iota(jnp.int32, rows[0].shape, 0)
    sums = []
    for here, beside in ((rows[0], above + rows[1]), (rows[1], rows[0] + below)):
        both = here + 0.5 * beside
        left = pltpu.roll(both, 1, 1)
        left = jnp.where(lane == 0, jnp.where(chunk == 0, 0.0, pltpu.roll(left, 1, 0)), left)
        right = pltpu.roll(both, LANES - 1, 1)
        right = jnp.where(
            lane == LANES - 1,
            jnp.where(chunk == chunks - 1, 0.0, pltpu.roll(right, chunks - 1, 0)),
            right,
        )
        sums.append(beside + left + right)
    return sums


def two_parts(values):
    high = values.astype(jnp.bfloat16)
    low = (values - high.astype(jnp.float32)).astype(jnp.bfloat16)
    return high, low


def kernel(
    n_sec, n_tile, disp_in, stiff_in, wgt_in, off_in, srow_in, scol_in, trow_in, tcol_in, cnt_in,
    out,
    disp, stiff, wgt, off, rows, cols, cnt, load_sem,
    field, force, total, inv, lhs, hot_lo, hot_hi, hi_ids, edge, halo, mine, theirs, weights,
    edge_send, edge_recv, val_send, val_recv, wgt_send, wgt_recv,
):
    sec = lax.axis_index("sec")
    tile = lax.axis_index("tile")
    chunks = field.shape[2]
    nodes_hi = 2 * chunks
    slots = wgt.shape[2]
    has_tile = [tile > 0, None, tile < n_tile - 1]
    first_role = jnp.where(sec < n_sec - 1, 0, 1)
    end_role = jnp.where(sec > 0, 2, 1)
    sides = ((0, 0), (2, 1))

    def when_tile(g, body):
        if has_tile[g] is None:
            body()
        else:
            pl.when(has_tile[g])(body)

    def each_role(body):
        def turn(role, carry):
            body(role)
            return carry

        lax.fori_loop(first_role, end_role, turn, jnp.int32(0))

    barrier = pltpu.get_barrier_semaphore()

    def greet(s, t):
        pl.semaphore_signal(barrier, inc=1, device_id=(s, t), device_id_type=MESH)

    for g in (0, 2):
        when_tile(g, lambda g=g: greet(sec, tile + g - 1))
    def greet_role(role):
        for g in (0, 2, 1):
            when_tile(g, lambda g=g: greet(sec + 1 - 2 * role, tile + g - 1))

    each_role(greet_role)

    low_side = jnp.where(tile > 0, 1, 0)
    high_side = jnp.where(tile < n_tile - 1, 1, 0)
    secs = jnp.where(sec > 0, 1, 0) + jnp.where(sec < n_sec - 1, 1, 0)
    greetings = low_side + high_side + secs * (1 + low_side + high_side)

    loads = [
        pltpu.make_async_copy(source, target, load_sem.at[i])
        for i, (source, target) in enumerate(
            (
                (disp_in, disp),
                (stiff_in, stiff),
                (scol_in, cols.at[0]),
                (srow_in, rows.at[0]),
                (tcol_in, cols.at[1]),
                (trow_in, rows.at[1]),
                (off_in, off.at[0]),
                (wgt_in, wgt),
                (cnt_in, cnt),
            )
        )
    ]
    for load in loads:
        load.start()

    def edge_copy(step, side, k, landed=False):
        to_side = side if landed else 1 - side
        return pltpu.make_async_remote_copy(
            src_ref=edge.at[step, side, k],
            dst_ref=halo.at[step, to_side, k],
            send_sem=edge_send.at[step, side, k],
            recv_sem=edge_recv.at[step, to_side, k],
            device_id=(sec, tile + 2 * side - 1),
            device_id_type=MESH,
        )

    def value_copy(step, role, g, landed=False):
        to_role, to_g = (role, g) if landed else (1 - role, 2 - g)
        return pltpu.make_async_remote_copy(
            src_ref=mine.at[step, role, g],
            dst_ref=theirs.at[step, to_role, to_g],
            send_sem=val_send.at[step, role, g],
            recv_sem=val_recv.at[step, to_role, to_g],
            device_id=(sec + 1 - 2 * role, tile + g - 1),
            device_id_type=MESH,
        )

    def weight_copy(g, landed=False):
        role = 1 if landed else 0
        to_g = g if landed else 2 - g
        return pltpu.make_async_remote_copy(
            src_ref=weights.at[0, g],
            dst_ref=weights.at[1, to_g],
            send_sem=wgt_send.at[g],
            recv_sem=wgt_recv.at[to_g],
            device_id=(sec + 1 - 2 * role, tile + g - 1),
            device_id_type=MESH,
        )

    def send_edges(step, k):
        for g, side in sides:
            pl.when(has_tile[g])(lambda side=side: edge_copy(step, side, k).start())

    def await_edges(step, k):
        for g, side in sides:
            pl.when(has_tile[g])(lambda side=side: edge_copy(step, side, k, True).wait_recv())

    for g, side in sides:

        @pl.when(jnp.logical_not(has_tile[g]))
        def _(g=g, side=side):
            halo[:, side] = jnp.zeros((STEPS,) + halo.shape[2:], jnp.float32)
            for role in range(2):
                weights[role, g] = jnp.zeros(weights.shape[2:], jnp.float32)
                for step in range(STEPS):
                    theirs[step, role, g] = jnp.zeros(theirs.shape[3:], jnp.float32)

    lane_slot = lax.broadcasted_iota(jnp.int32, (1, slots), 1)
    lo_node = lax.broadcasted_iota(jnp.int32, (LANES, slots), 0)
    hi_node = lax.broadcasted_iota(jnp.int32, (nodes_hi, slots), 0)

    loads[0].wait()
    loads[1].wait()
    for r in range(2):
        c_row = stiff[pl.ds(r, chunks, stride=2), :]
        edge[0, r, 2] = c_row
        for k in range(2):
            u_row = disp[k, pl.ds(r, chunks, stride=2), :]
            field[k, r] = u_row
            edge[0, r, k] = c_row * u_row

    for load in loads[2:]:
        load.wait()

    off[1] = jnp.zeros(off.shape[1:], jnp.float32)

    @pl.when(sec < n_sec - 1)
    def _():
        for g in range(3):

            def mask(g=g):
                weights[0, g] = jnp.where(lane_slot < cnt[:, g : g + 1], wgt[g], 0.0)

            when_tile(g, mask)

    def prepare(role):
        for g in range(3):
            col = cols[role, g]
            hi = rows[role, g] * chunks + (col >> 7)
            hi_ids[role, g] = hi
            at = pl.ds(g * slots, slots)
            hot = jnp.where(lo_node == (col & (LANES - 1)), 1.0, 0.0).astype(jnp.bfloat16)
            hot_lo[role, pl.ds(0, LANES), at] = hot
            hot_lo[role, pl.ds(LANES, LANES), at] = hot
            hot_hi[role, :, at] = jnp.where(hi_node == hi, 1.0, 0.0).astype(jnp.bfloat16)

    each_role(prepare)

    def pick(step, role):
        for g in (0, 2, 1):
            found = jnp.dot(
                lhs[...],
                hot_lo[role, :, pl.ds(g * slots, slots)],
                preferred_element_type=jnp.float32,
            )
            hit = hi_node == hi_ids[role, g]
            for k in range(2):
                value = jnp.sum(
                    jnp.where(hit, found[k * nodes_hi : (k + 1) * nodes_hi], 0.0),
                    axis=0,
                    keepdims=True,
                )
                mine[step, role, g, pl.ds(k, 1), :] = value - off[role, g, pl.ds(k, 1), :]

    def send_values(step, role):
        for g in (0, 2, 1):
            when_tile(g, lambda g=g: value_copy(step, role, g).start())

    def spread(role, g, values):
        at = pl.ds(g * slots, slots)
        high = [row.astype(jnp.bfloat16) for row in values]
        low = [(row - h.astype(jnp.float32)).astype(jnp.bfloat16) for row, h in zip(values, high)]
        summed = lax.dot_general(
            jnp.concatenate([hot_hi[role, :, at] * part for part in high + low], axis=0),
            hot_lo[role, pl.ds(0, LANES), at],
            (((1,), (1,)), ((), ())),
            preferred_element_type=jnp.float32,
        )
        half = len(values) * nodes_hi
        return summed[:half] + summed[half:]

    def drain(step):
        def drain_role(role):
            for g in range(3):
                when_tile(g, lambda g=g: value_copy(step, role, g).wait_send())

        each_role(drain_role)
        if step == 0:

            @pl.when(sec < n_sec - 1)
            def _():
                for g in range(3):
                    when_tile(g, lambda g=g: weight_copy(g).wait_send())

        for g, side in sides:

            @pl.when(has_tile[g])
            def _(side=side):
                for k in range(3 if step == 0 else 2):
                    edge_copy(step, side, k).wait_send()

    for step in range(STEPS):
        for k in range(2):
            part = two_parts(field[k].reshape(nodes_hi, LANES))
            lhs[pl.ds(k * nodes_hi, nodes_hi), pl.ds(0, LANES)] = part[0]
            lhs[pl.ds(k * nodes_hi, nodes_hi), pl.ds(LANES, LANES)] = part[1]
        each_role(functools.partial(pick, step))
        if step == 0:
            pl.semaphore_wait(barrier, greetings)
        each_role(functools.partial(send_values, step))
        if step == 0:

            @pl.when(sec < n_sec - 1)
            def _():
                for g in (0, 2, 1):
                    when_tile(g, lambda g=g: weight_copy(g).start())

            send_edges(0, 0)
            send_edges(0, 2)
        send_edges(step, 1)
        if step > 0:
            drain(step - 1)

        if step == 0:
            inv[...] = jnp.zeros(inv.shape, jnp.float32)

        force[...] = jnp.zeros(force.shape, jnp.float32)

        def spread_pulls(role, step=step):
            for batch in ((1,), (0, 2)):
                if step == 0:

                    @pl.when(role == 1)
                    def _(batch=batch):
                        for g in batch:
                            when_tile(g, lambda g=g: weight_copy(g, True).wait_recv())

                for g in batch:
                    when_tile(g, lambda g=g: value_copy(step, role, g, True).wait_recv())
                at = 0.0
                for g in batch:
                    weight = weights[role, g]
                    pull = weight * (theirs[step, role, g] - mine[step, role, g])
                    values = [pull[0:1], pull[1:2]] + ([weight] if step == 0 else [])
                    at = at + spread(role, g, values)
                force[...] += at[: 2 * nodes_hi].reshape(force.shape)
                if step == 0:
                    inv[...] += at[2 * nodes_hi :].reshape(inv.shape)

        each_role(spread_pulls)

        if step == 0:
            await_edges(0, 2)
            c_rows = [edge[0, r, 2] for r in range(2)]
            sums = stencil(c_rows, halo[0, 0, 2], halo[0, 1, 2])
            for r in range(2):
                springs = c_rows[r] * sums[r]
                total[r] = springs
                inv[r] = DAMPING / (inv[r] + springs)

        for k in range(2):
            await_edges(step, k)
            sums = stencil([edge[step, r, k] for r in range(2)], halo[step, 0, k], halo[step, 1, k])
            for r in range(2):
                c_row = edge[0, r, 2]
                here = field[k, r]
                pulled = force[k, r] + c_row * sums[r] - here * total[r]
                new = here + pulled * inv[r]
                if step < STEPS - 1:
                    field[k, r] = new
                    edge[step + 1, r, k] = c_row * new
                else:
                    out[k, pl.ds(r, chunks, stride=2), :] = new
            if step < STEPS - 1 and k == 0:
                send_edges(step + 1, 0)

    drain(STEPS - 1)


def relax(n_sec, n_tile, *args):
    displacement, stiffness, weight, offset, srow, scol, trow, tcol, count = args
    rows, width = stiffness.shape[1:]
    slots = weight.shape[2]
    chunks = width // LANES
    nodes_hi = rows * chunks

    def interleaved(x):
        x = x.reshape(-1, rows, chunks, LANES).transpose(0, 2, 1, 3)
        return x.reshape(-1, nodes_hi, LANES)

    operands = (
        interleaved(displacement), interleaved(stiffness)[0], weight.transpose(1, 0, 2),
        offset[0].transpose(1, 0, 2), srow.transpose(1, 0, 2), scol.transpose(1, 0, 2),
        trow.transpose(1, 0, 2), tcol.transpose(1, 0, 2), count,
    )
    vmem = pl.BlockSpec(memory_space=pltpu.VMEM)
    dma = pltpu.SemaphoreType.DMA
    f32 = jnp.float32
    out = pl.pallas_call(
        functools.partial(kernel, n_sec, n_tile),
        out_shape=jax.ShapeDtypeStruct((2, nodes_hi, LANES), f32),
        in_specs=[pl.BlockSpec(memory_space=pltpu.HBM)] * 9,
        out_specs=vmem,
        scratch_shapes=[
            pltpu.VMEM((2, nodes_hi, LANES), f32),
            pltpu.VMEM((nodes_hi, LANES), f32),
            pltpu.VMEM((3, 1, slots), f32),
            pltpu.VMEM((2, 3, 2, slots), f32),
            pltpu.VMEM((2, 3, 1, slots), jnp.int32),
            pltpu.VMEM((2, 3, 1, slots), jnp.int32),
            pltpu.VMEM((1, 3), jnp.int32),
            dma((9,)),
            pltpu.VMEM((2, rows, chunks, LANES), f32),
            pltpu.VMEM((2, rows, chunks, LANES), f32),
            pltpu.VMEM((rows, chunks, LANES), f32),
            pltpu.VMEM((rows, chunks, LANES), f32),
            pltpu.VMEM((2 * nodes_hi, 2 * LANES), jnp.bfloat16),
            pltpu.VMEM((2, 2 * LANES, 3 * slots), jnp.bfloat16),
            pltpu.VMEM((2, nodes_hi, 3 * slots), jnp.bfloat16),
            pltpu.VMEM((2, 3, 1, slots), jnp.int32),
            pltpu.VMEM((STEPS, 2, 3, chunks, LANES), f32),
            pltpu.VMEM((STEPS, 2, 3, chunks, LANES), f32),
            pltpu.VMEM((STEPS, 2, 3, 2, slots), f32),
            pltpu.VMEM((STEPS, 2, 3, 2, slots), f32),
            pltpu.VMEM((2, 3, 1, slots), f32),
            dma((STEPS, 2, 3)),
            dma((STEPS, 2, 3)),
            dma((STEPS, 2, 3)),
            dma((STEPS, 2, 3)),
            dma((3,)),
            dma((3,)),
        ],
        compiler_params=pltpu.CompilerParams(
            collective_id=0, has_side_effects=True, vmem_limit_bytes=24 * 1024 * 1024
        ),
    )(*[pltpu.with_memory_space_constraint(x, pltpu.HBM) for x in operands])
    out = out.reshape(2, chunks, rows, LANES).transpose(0, 2, 1, 3)
    return out.reshape(1, 2, rows, width)


def solution(mesh):
    placed = (
        P("sec", None, "tile", None),
        P("sec", "tile", None),
        P("sec", "tile", None),
        P("sec", None, "tile", None),
        P("sec", "tile", None),
        P("sec", "tile", None),
        P("sec", "tile", None),
        P("sec", "tile", None),
        P("sec", "tile"),
    )
    return jax.shard_map(
        functools.partial(relax, mesh.shape["sec"], mesh.shape["tile"]),
        mesh=mesh, in_specs=placed, out_specs=P("sec", None, "tile", None), check_vma=False,
    )
```

```python
import functools
import jax
import jax.numpy as jnp
from jax import lax
from jax.experimental import pallas as pl
from jax.experimental.pallas import tpu as pltpu
from jax.sharding import PartitionSpec as P

STEPS = 2
DAMPING = 0.7
LANES = 128
MESH = pl.DeviceIdType.MESH


def stencil(rows, above, below):
    chunks = rows[0].shape[0]
    lane = lax.broadcasted_iota(jnp.int32, rows[0].shape, 1)
    chunk = lax.broadcasted_iota(jnp.int32, rows[0].shape, 0)
    sums = []
    for here, beside in ((rows[0], above + rows[1]), (rows[1], rows[0] + below)):
        both = here + 0.5 * beside
        left = pltpu.roll(both, 1, 1)
        left = jnp.where(lane == 0, jnp.where(chunk == 0, 0.0, pltpu.roll(left, 1, 0)), left)
        right = pltpu.roll(both, LANES - 1, 1)
        right = jnp.where(
            lane == LANES - 1,
            jnp.where(chunk == chunks - 1, 0.0, pltpu.roll(right, chunks - 1, 0)),
            right,
        )
        sums.append(beside + left + right)
    return sums


def two_parts(values):
    high = values.astype(jnp.bfloat16)
    low = (values - high.astype(jnp.float32)).astype(jnp.bfloat16)
    return high, low


def kernel(
    n_sec, n_tile, disp_in, stiff_in, wgt_in, off_in, srow_in, scol_in, trow_in, tcol_in, cnt_in,
    out,
    disp, stiff, wgt, off, rows, cols, cnt, load_sem,
    field, force, total, inv, lhs, hot_lo, hot_hi, hi_ids, edge, halo, mine, theirs, weights,
    edge_send, edge_recv, val_send, val_recv, wgt_send, wgt_recv,
):
    sec = lax.axis_index("sec")
    tile = lax.axis_index("tile")
    chunks = field.shape[2]
    nodes_hi = 2 * chunks
    slots = wgt.shape[2]
    has_tile = [tile > 0, None, tile < n_tile - 1]
    first_role = jnp.where(sec < n_sec - 1, 0, 1)
    end_role = jnp.where(sec > 0, 2, 1)
    sides = ((0, 0), (2, 1))

    def when_tile(g, body):
        if has_tile[g] is None:
            body()
        else:
            pl.when(has_tile[g])(body)

    def each_role(body):
        def turn(role, carry):
            body(role)
            return carry

        lax.fori_loop(first_role, end_role, turn, jnp.int32(0))

    barrier = pltpu.get_barrier_semaphore()

    def greet(s, t):
        pl.semaphore_signal(barrier, inc=1, device_id=(s, t), device_id_type=MESH)

    for g in (0, 2):
        when_tile(g, lambda g=g: greet(sec, tile + g - 1))
    def greet_role(role):
        for g in (0, 2, 1):
            when_tile(g, lambda g=g: greet(sec + 1 - 2 * role, tile + g - 1))

    each_role(greet_role)

    low_side = jnp.where(tile > 0, 1, 0)
    high_side = jnp.where(tile < n_tile - 1, 1, 0)
    secs = jnp.where(sec > 0, 1, 0) + jnp.where(sec < n_sec - 1, 1, 0)
    greetings = low_side + high_side + secs * (1 + low_side + high_side)

    loads = [
        pltpu.make_async_copy(source, target, load_sem.at[i])
        for i, (source, target) in enumerate(
            (
                (disp_in, disp),
                (stiff_in, stiff),
                (scol_in, cols.at[0]),
                (srow_in, rows.at[0]),
                (tcol_in, cols.at[1]),
                (trow_in, rows.at[1]),
                (off_in, off.at[0]),
                (wgt_in, wgt),
                (cnt_in, cnt),
            )
        )
    ]
    for load in loads:
        load.start()

    def edge_copy(step, side, k, landed=False):
        to_side = side if landed else 1 - side
        return pltpu.make_async_remote_copy(
            src_ref=edge.at[step, side, k],
            dst_ref=halo.at[step, to_side, k],
            send_sem=edge_send.at[step, side, k],
            recv_sem=edge_recv.at[step, to_side, k],
            device_id=(sec, tile + 2 * side - 1),
            device_id_type=MESH,
        )

    def value_copy(step, role, g, landed=False):
        to_role, to_g = (role, g) if landed else (1 - role, 2 - g)
        return pltpu.make_async_remote_copy(
            src_ref=mine.at[step, role, g],
            dst_ref=theirs.at[step, to_role, to_g],
            send_sem=val_send.at[step, role, g],
            recv_sem=val_recv.at[step, to_role, to_g],
            device_id=(sec + 1 - 2 * role, tile + g - 1),
            device_id_type=MESH,
        )

    def weight_copy(g, landed=False):
        role = 1 if landed else 0
        to_g = g if landed else 2 - g
        return pltpu.make_async_remote_copy(
            src_ref=weights.at[0, g],
            dst_ref=weights.at[1, to_g],
            send_sem=wgt_send.at[g],
            recv_sem=wgt_recv.at[to_g],
            device_id=(sec + 1 - 2 * role, tile + g - 1),
            device_id_type=MESH,
        )

    def send_edges(step, k):
        for g, side in sides:
            pl.when(has_tile[g])(lambda side=side: edge_copy(step, side, k).start())

    def await_edges(step, k):
        for g, side in sides:
            pl.when(has_tile[g])(lambda side=side: edge_copy(step, side, k, True).wait_recv())

    for g, side in sides:

        @pl.when(jnp.logical_not(has_tile[g]))
        def _(g=g, side=side):
            halo[:, side] = jnp.zeros((STEPS,) + halo.shape[2:], jnp.float32)
            for role in range(2):
                weights[role, g] = jnp.zeros(weights.shape[2:], jnp.float32)
                for step in range(STEPS):
                    theirs[step, role, g] = jnp.zeros(theirs.shape[3:], jnp.float32)

    lane_slot = lax.broadcasted_iota(jnp.int32, (1, slots), 1)
    lo_node = lax.broadcasted_iota(jnp.int32, (LANES, slots), 0)
    hi_node = lax.broadcasted_iota(jnp.int32, (nodes_hi, slots), 0)

    loads[0].wait()
    loads[1].wait()
    for r in range(2):
        c_row = stiff[pl.ds(r, chunks, stride=2), :]
        edge[0, r, 2] = c_row
        for k in range(2):
            u_row = disp[k, pl.ds(r, chunks, stride=2), :]
            field[k, r] = u_row
            edge[0, r, k] = c_row * u_row

    for load in loads[2:]:
        load.wait()

    off[1] = jnp.zeros(off.shape[1:], jnp.float32)

    @pl.when(sec < n_sec - 1)
    def _():
        for g in range(3):

            def mask(g=g):
                weights[0, g] = jnp.where(lane_slot < cnt[:, g : g + 1], wgt[g], 0.0)

            when_tile(g, mask)

    def prepare(role):
        for g in range(3):
            col = cols[role, g]
            hi = rows[role, g] * chunks + (col >> 7)
            hi_ids[role, g] = hi
            at = pl.ds(g * slots, slots)
            hot = jnp.where(lo_node == (col & (LANES - 1)), 1.0, 0.0).astype(jnp.bfloat16)
            hot_lo[role, pl.ds(0, LANES), at] = hot
            hot_lo[role, pl.ds(LANES, LANES), at] = hot
            hot_hi[role, :, at] = jnp.where(hi_node == hi, 1.0, 0.0).astype(jnp.bfloat16)

    each_role(prepare)

    def pick(step, comps, role):
        start, count = comps[0] * nodes_hi, len(comps) * nodes_hi
        for g in (0, 2, 1):
            found = jnp.dot(
                lhs[pl.ds(start, count)],
                hot_lo[role, :, pl.ds(g * slots, slots)],
                preferred_element_type=jnp.float32,
            )
            hit = hi_node == hi_ids[role, g]
            for i, k in enumerate(comps):
                value = jnp.sum(
                    jnp.where(hit, found[i * nodes_hi : (i + 1) * nodes_hi], 0.0),
                    axis=0,
                    keepdims=True,
                )
                mine[step, role, g, pl.ds(k, 1), :] = value - off[role, g, pl.ds(k, 1), :]

    def pick_all(step, comps):
        for k in comps:
            high, low = two_parts(field[k].reshape(nodes_hi, LANES))
            lhs[pl.ds(k * nodes_hi, nodes_hi), pl.ds(0, LANES)] = high
            lhs[pl.ds(k * nodes_hi, nodes_hi), pl.ds(LANES, LANES)] = low
        each_role(functools.partial(pick, step, comps))

    def send_values(step, role):
        for g in (0, 2, 1):
            when_tile(g, lambda g=g: value_copy(step, role, g).start())

    def spread(role, g, values):
        at = pl.ds(g * slots, slots)
        high = [row.astype(jnp.bfloat16) for row in values]
        low = [(row - h.astype(jnp.float32)).astype(jnp.bfloat16) for row, h in zip(values, high)]
        summed = lax.dot_general(
            jnp.concatenate([hot_hi[role, :, at] * part for part in high + low], axis=0),
            hot_lo[role, pl.ds(0, LANES), at],
            (((1,), (1,)), ((), ())),
            preferred_element_type=jnp.float32,
        )
        half = len(values) * nodes_hi
        return summed[:half] + summed[half:]

    def drain(step):
        def drain_role(role):
            for g in range(3):
                when_tile(g, lambda g=g: value_copy(step, role, g).wait_send())

        each_role(drain_role)
        if step == 0:

            @pl.when(sec < n_sec - 1)
            def _():
                for g in range(3):
                    when_tile(g, lambda g=g: weight_copy(g).wait_send())

        for g, side in sides:

            @pl.when(has_tile[g])
            def _(side=side):
                for k in range(3 if step == 0 else 2):
                    edge_copy(step, side, k).wait_send()

    for step in range(STEPS):
        if step == 0:
            pick_all(0, (0, 1))
        if step == 0:
            pl.semaphore_wait(barrier, greetings)
        each_role(functools.partial(send_values, step))
        if step == 0:

            @pl.when(sec < n_sec - 1)
            def _():
                for g in (0, 2, 1):
                    when_tile(g, lambda g=g: weight_copy(g).start())

            send_edges(0, 0)
            send_edges(0, 2)
        send_edges(step, 1)
        if step > 0:
            drain(step - 1)

        if step == 0:
            inv[...] = jnp.zeros(inv.shape, jnp.float32)

        force[...] = jnp.zeros(force.shape, jnp.float32)

        def spread_pulls(role, step=step):
            for batch in ((1,), (0, 2)):
                if step == 0:

                    @pl.when(role == 1)
                    def _(batch=batch):
                        for g in batch:
                            when_tile(g, lambda g=g: weight_copy(g, True).wait_recv())

                for g in batch:
                    when_tile(g, lambda g=g: value_copy(step, role, g, True).wait_recv())
                at = 0.0
                for g in batch:
                    weight = weights[role, g]
                    pull = weight * (theirs[step, role, g] - mine[step, role, g])
                    values = [pull[0:1], pull[1:2]] + ([weight] if step == 0 else [])
                    at = at + spread(role, g, values)
                force[...] += at[: 2 * nodes_hi].reshape(force.shape)
                if step == 0:
                    inv[...] += at[2 * nodes_hi :].reshape(inv.shape)

        each_role(spread_pulls)

        if step == 0:
            await_edges(0, 2)
            c_rows = [edge[0, r, 2] for r in range(2)]
            sums = stencil(c_rows, halo[0, 0, 2], halo[0, 1, 2])
            for r in range(2):
                springs = c_rows[r] * sums[r]
                total[r] = springs
                inv[r] = DAMPING / (inv[r] + springs)

        for k in range(2):
            await_edges(step, k)
            sums = stencil([edge[step, r, k] for r in range(2)], halo[step, 0, k], halo[step, 1, k])
            for r in range(2):
                c_row = edge[0, r, 2]
                here = field[k, r]
                pulled = force[k, r] + c_row * sums[r] - here * total[r]
                new = here + pulled * inv[r]
                if step < STEPS - 1:
                    field[k, r] = new
                    edge[step + 1, r, k] = c_row * new
                else:
                    out[k, pl.ds(r, chunks, stride=2), :] = new
            if step < STEPS - 1:
                if k == 0:
                    send_edges(step + 1, 0)
                pick_all(step + 1, (k,))

    drain(STEPS - 1)


def relax(n_sec, n_tile, *args):
    displacement, stiffness, weight, offset, srow, scol, trow, tcol, count = args
    rows, width = stiffness.shape[1:]
    slots = weight.shape[2]
    chunks = width // LANES
    nodes_hi = rows * chunks

    def interleaved(x):
        x = x.reshape(-1, rows, chunks, LANES).transpose(0, 2, 1, 3)
        return x.reshape(-1, nodes_hi, LANES)

    operands = (
        interleaved(displacement), interleaved(stiffness)[0], weight.transpose(1, 0, 2),
        offset[0].transpose(1, 0, 2), srow.transpose(1, 0, 2), scol.transpose(1, 0, 2),
        trow.transpose(1, 0, 2), tcol.transpose(1, 0, 2), count,
    )
    vmem = pl.BlockSpec(memory_space=pltpu.VMEM)
    dma = pltpu.SemaphoreType.DMA
    f32 = jnp.float32
    out = pl.pallas_call(
        functools.partial(kernel, n_sec, n_tile),
        out_shape=jax.ShapeDtypeStruct((2, nodes_hi, LANES), f32),
        in_specs=[pl.BlockSpec(memory_space=pltpu.HBM)] * 9,
        out_specs=vmem,
        scratch_shapes=[
            pltpu.VMEM((2, nodes_hi, LANES), f32),
            pltpu.VMEM((nodes_hi, LANES), f32),
            pltpu.VMEM((3, 1, slots), f32),
            pltpu.VMEM((2, 3, 2, slots), f32),
            pltpu.VMEM((2, 3, 1, slots), jnp.int32),
            pltpu.VMEM((2, 3, 1, slots), jnp.int32),
            pltpu.VMEM((1, 3), jnp.int32),
            dma((9,)),
            pltpu.VMEM((2, rows, chunks, LANES), f32),
            pltpu.VMEM((2, rows, chunks, LANES), f32),
            pltpu.VMEM((rows, chunks, LANES), f32),
            pltpu.VMEM((rows, chunks, LANES), f32),
            pltpu.VMEM((2 * nodes_hi, 2 * LANES), jnp.bfloat16),
            pltpu.VMEM((2, 2 * LANES, 3 * slots), jnp.bfloat16),
            pltpu.VMEM((2, nodes_hi, 3 * slots), jnp.bfloat16),
            pltpu.VMEM((2, 3, 1, slots), jnp.int32),
            pltpu.VMEM((STEPS, 2, 3, chunks, LANES), f32),
            pltpu.VMEM((STEPS, 2, 3, chunks, LANES), f32),
            pltpu.VMEM((STEPS, 2, 3, 2, slots), f32),
            pltpu.VMEM((STEPS, 2, 3, 2, slots), f32),
            pltpu.VMEM((2, 3, 1, slots), f32),
            dma((STEPS, 2, 3)),
            dma((STEPS, 2, 3)),
            dma((STEPS, 2, 3)),
            dma((STEPS, 2, 3)),
            dma((3,)),
            dma((3,)),
        ],
        compiler_params=pltpu.CompilerParams(
            collective_id=0, has_side_effects=True, vmem_limit_bytes=24 * 1024 * 1024
        ),
    )(*[pltpu.with_memory_space_constraint(x, pltpu.HBM) for x in operands])
    out = out.reshape(2, chunks, rows, LANES).transpose(0, 2, 1, 3)
    return out.reshape(1, 2, rows, width)


def solution(mesh):
    placed = (
        P("sec", None, "tile", None),
        P("sec", "tile", None),
        P("sec", "tile", None),
        P("sec", None, "tile", None),
        P("sec", "tile", None),
        P("sec", "tile", None),
        P("sec", "tile", None),
        P("sec", "tile", None),
        P("sec", "tile"),
    )
    return jax.shard_map(
        functools.partial(relax, mesh.shape["sec"], mesh.shape["tile"]),
        mesh=mesh, in_specs=placed, out_specs=P("sec", None, "tile", None), check_vma=False,
    )
```

```python
import functools
import jax
import jax.numpy as jnp
from jax import lax
from jax.experimental import pallas as pl
from jax.experimental.pallas import tpu as pltpu
from jax.sharding import PartitionSpec as P

STEPS = 2
DAMPING = 0.7
LANES = 128
MESH = pl.DeviceIdType.MESH


def stencil(rows, above, below):
    chunks = rows[0].shape[0]
    lane = lax.broadcasted_iota(jnp.int32, rows[0].shape, 1)
    chunk = lax.broadcasted_iota(jnp.int32, rows[0].shape, 0)
    sums = []
    for here, beside in ((rows[0], above + rows[1]), (rows[1], rows[0] + below)):
        both = here + 0.5 * beside
        left = pltpu.roll(both, 1, 1)
        left = jnp.where(lane == 0, jnp.where(chunk == 0, 0.0, pltpu.roll(left, 1, 0)), left)
        right = pltpu.roll(both, LANES - 1, 1)
        right = jnp.where(
            lane == LANES - 1,
            jnp.where(chunk == chunks - 1, 0.0, pltpu.roll(right, chunks - 1, 0)),
            right,
        )
        sums.append(beside + left + right)
    return sums


def kernel(
    n_sec, n_tile, disp_in, stiff_in, wgt_in, off_in, srow_in, scol_in, trow_in, tcol_in, cnt_in,
    out,
    disp, stiff, wgt, off, rows, cols, cnt, load_sem,
    field, force, total, inv, hot_lo, hot_hi, hi_ids, edge, halo, mine, theirs, weights,
    edge_send, edge_recv, val_send, val_recv, wgt_send, wgt_recv,
):
    sec = lax.axis_index("sec")
    tile = lax.axis_index("tile")
    chunks = field.shape[2]
    nodes_hi = 2 * chunks
    slots = wgt.shape[2]
    has_tile = [tile > 0, None, tile < n_tile - 1]
    first_role = jnp.where(sec < n_sec - 1, 0, 1)
    end_role = jnp.where(sec > 0, 2, 1)
    sides = ((0, 0), (2, 1))

    def when_tile(g, body):
        if has_tile[g] is None:
            body()
        else:
            pl.when(has_tile[g])(body)

    def each_role(body):
        def turn(role, carry):
            body(role)
            return carry

        lax.fori_loop(first_role, end_role, turn, jnp.int32(0))

    barrier = pltpu.get_barrier_semaphore()

    def greet(s, t):
        pl.semaphore_signal(barrier, inc=1, device_id=(s, t), device_id_type=MESH)

    for g in (0, 2):
        when_tile(g, lambda g=g: greet(sec, tile + g - 1))
    def greet_role(role):
        for g in (0, 2, 1):
            when_tile(g, lambda g=g: greet(sec + 1 - 2 * role, tile + g - 1))

    each_role(greet_role)

    low_side = jnp.where(tile > 0, 1, 0)
    high_side = jnp.where(tile < n_tile - 1, 1, 0)
    secs = jnp.where(sec > 0, 1, 0) + jnp.where(sec < n_sec - 1, 1, 0)
    greetings = low_side + high_side + secs * (1 + low_side + high_side)

    loads = [
        pltpu.make_async_copy(source, target, load_sem.at[i])
        for i, (source, target) in enumerate(
            (
                (disp_in, disp),
                (stiff_in, stiff),
                (scol_in, cols.at[0]),
                (srow_in, rows.at[0]),
                (tcol_in, cols.at[1]),
                (trow_in, rows.at[1]),
                (off_in, off.at[0]),
                (wgt_in, wgt),
                (cnt_in, cnt),
            )
        )
    ]
    for load in loads:
        load.start()

    def edge_copy(step, side, k, landed=False):
        to_side = side if landed else 1 - side
        return pltpu.make_async_remote_copy(
            src_ref=edge.at[step, side, k],
            dst_ref=halo.at[step, to_side, k],
            send_sem=edge_send.at[step, side, k],
            recv_sem=edge_recv.at[step, to_side, k],
            device_id=(sec, tile + 2 * side - 1),
            device_id_type=MESH,
        )

    def value_copy(step, role, g, landed=False):
        to_role, to_g = (role, g) if landed else (1 - role, 2 - g)
        return pltpu.make_async_remote_copy(
            src_ref=mine.at[step, role, g],
            dst_ref=theirs.at[step, to_role, to_g],
            send_sem=val_send.at[step, role, g],
            recv_sem=val_recv.at[step, to_role, to_g],
            device_id=(sec + 1 - 2 * role, tile + g - 1),
            device_id_type=MESH,
        )

    def weight_copy(g, landed=False):
        role = 1 if landed else 0
        to_g = g if landed else 2 - g
        return pltpu.make_async_remote_copy(
            src_ref=weights.at[0, g],
            dst_ref=weights.at[1, to_g],
            send_sem=wgt_send.at[g],
            recv_sem=wgt_recv.at[to_g],
            device_id=(sec + 1 - 2 * role, tile + g - 1),
            device_id_type=MESH,
        )

    def send_edges(step, k):
        for g, side in sides:
            pl.when(has_tile[g])(lambda side=side: edge_copy(step, side, k).start())

    def await_edges(step, k):
        for g, side in sides:
            pl.when(has_tile[g])(lambda side=side: edge_copy(step, side, k, True).wait_recv())

    for g, side in sides:

        @pl.when(jnp.logical_not(has_tile[g]))
        def _(g=g, side=side):
            halo[:, side] = jnp.zeros((STEPS,) + halo.shape[2:], jnp.float32)
            for role in range(2):
                weights[role, g] = jnp.zeros(weights.shape[2:], jnp.float32)
                for step in range(STEPS):
                    theirs[step, role, g] = jnp.zeros(theirs.shape[3:], jnp.float32)

    lane_slot = lax.broadcasted_iota(jnp.int32, (1, slots), 1)
    lo_node = lax.broadcasted_iota(jnp.int32, (LANES, slots), 0)
    hi_node = lax.broadcasted_iota(jnp.int32, (nodes_hi, slots), 0)

    loads[0].wait()
    loads[1].wait()
    for r in range(2):
        c_row = stiff[pl.ds(r, chunks, stride=2), :]
        edge[0, r, 2] = c_row
        for k in range(2):
            u_row = disp[k, pl.ds(r, chunks, stride=2), :]
            field[k, r] = u_row
            edge[0, r, k] = c_row * u_row

    for load in loads[2:]:
        load.wait()

    off[1] = jnp.zeros(off.shape[1:], jnp.float32)

    @pl.when(sec < n_sec - 1)
    def _():
        for g in range(3):

            def mask(g=g):
                weights[0, g] = jnp.where(lane_slot < cnt[:, g : g + 1], wgt[g], 0.0)

            when_tile(g, mask)

    def prepare(role):
        for g in range(3):
            col = cols[role, g]
            hi = rows[role, g] * chunks + (col >> 7)
            hi_ids[role, g] = hi
            at = pl.ds(g * slots, slots)
            hot = jnp.where(lo_node == (col & (LANES - 1)), 1.0, 0.0).astype(jnp.bfloat16)
            hot_lo[role, :, at] = hot
            hot_hi[role, :, at] = jnp.where(hi_node == hi, 1.0, 0.0).astype(jnp.bfloat16)

    each_role(prepare)

    def pick(step, role):
        fields = [field[k].reshape(nodes_hi, LANES) for k in range(2)]
        for g in (0, 2, 1):
            lo = cols[role, g] & (LANES - 1)
            hit = hi_node == hi_ids[role, g]
            for k in range(2):
                found = [
                    jnp.take_along_axis(
                        fields[k],
                        jnp.broadcast_to(lo[:, at : at + LANES], (nodes_hi, LANES)),
                        axis=1,
                        mode="promise_in_bounds",
                    )
                    for at in range(0, slots, LANES)
                ]
                value = jnp.sum(
                    jnp.where(hit, jnp.concatenate(found, axis=1), 0.0), axis=0, keepdims=True
                )
                mine[step, role, g, pl.ds(k, 1), :] = value - off[role, g, pl.ds(k, 1), :]

    def send_values(step, role):
        for g in (0, 2, 1):
            when_tile(g, lambda g=g: value_copy(step, role, g).start())

    def spread(role, g, values):
        at = pl.ds(g * slots, slots)
        high = [row.astype(jnp.bfloat16) for row in values]
        low = [(row - h.astype(jnp.float32)).astype(jnp.bfloat16) for row, h in zip(values, high)]
        summed = lax.dot_general(
            jnp.concatenate([hot_hi[role, :, at] * part for part in high + low], axis=0),
            hot_lo[role, :, at],
            (((1,), (1,)), ((), ())),
            preferred_element_type=jnp.float32,
        )
        half = len(values) * nodes_hi
        return summed[:half] + summed[half:]

    def drain(step):
        def drain_role(role):
            for g in range(3):
                when_tile(g, lambda g=g: value_copy(step, role, g).wait_send())

        each_role(drain_role)
        if step == 0:

            @pl.when(sec < n_sec - 1)
            def _():
                for g in range(3):
                    when_tile(g, lambda g=g: weight_copy(g).wait_send())

        for g, side in sides:

            @pl.when(has_tile[g])
            def _(side=side):
                for k in range(3 if step == 0 else 2):
                    edge_copy(step, side, k).wait_send()

    for step in range(STEPS):
        each_role(functools.partial(pick, step))
        if step == 0:
            pl.semaphore_wait(barrier, greetings)
        each_role(functools.partial(send_values, step))
        if step == 0:

            @pl.when(sec < n_sec - 1)
            def _():
                for g in (0, 2, 1):
                    when_tile(g, lambda g=g: weight_copy(g).start())

            send_edges(0, 0)
            send_edges(0, 2)
        send_edges(step, 1)
        if step > 0:
            drain(step - 1)

        if step == 0:
            inv[...] = jnp.zeros(inv.shape, jnp.float32)

        force[...] = jnp.zeros(force.shape, jnp.float32)

        def spread_pulls(role, step=step):
            for batch in ((1,), (0, 2)):
                if step == 0:

                    @pl.when(role == 1)
                    def _(batch=batch):
                        for g in batch:
                            when_tile(g, lambda g=g: weight_copy(g, True).wait_recv())

                for g in batch:
                    when_tile(g, lambda g=g: value_copy(step, role, g, True).wait_recv())
                at = 0.0
                for g in batch:
                    weight = weights[role, g]
                    pull = weight * (theirs[step, role, g] - mine[step, role, g])
                    values = [pull[0:1], pull[1:2]] + ([weight] if step == 0 else [])
                    at = at + spread(role, g, values)
                force[...] += at[: 2 * nodes_hi].reshape(force.shape)
                if step == 0:
                    inv[...] += at[2 * nodes_hi :].reshape(inv.shape)

        each_role(spread_pulls)

        if step == 0:
            await_edges(0, 2)
            c_rows = [edge[0, r, 2] for r in range(2)]
            sums = stencil(c_rows, halo[0, 0, 2], halo[0, 1, 2])
            for r in range(2):
                springs = c_rows[r] * sums[r]
                total[r] = springs
                inv[r] = DAMPING / (inv[r] + springs)

        for k in range(2):
            await_edges(step, k)
            sums = stencil([edge[step, r, k] for r in range(2)], halo[step, 0, k], halo[step, 1, k])
            for r in range(2):
                c_row = edge[0, r, 2]
                here = field[k, r]
                pulled = force[k, r] + c_row * sums[r] - here * total[r]
                new = here + pulled * inv[r]
                if step < STEPS - 1:
                    field[k, r] = new
                    edge[step + 1, r, k] = c_row * new
                else:
                    out[k, pl.ds(r, chunks, stride=2), :] = new
            if step < STEPS - 1 and k == 0:
                send_edges(step + 1, 0)

    drain(STEPS - 1)


def relax(n_sec, n_tile, *args):
    displacement, stiffness, weight, offset, srow, scol, trow, tcol, count = args
    rows, width = stiffness.shape[1:]
    slots = weight.shape[2]
    chunks = width // LANES
    nodes_hi = rows * chunks

    def interleaved(x):
        x = x.reshape(-1, rows, chunks, LANES).transpose(0, 2, 1, 3)
        return x.reshape(-1, nodes_hi, LANES)

    operands = (
        interleaved(displacement), interleaved(stiffness)[0], weight.transpose(1, 0, 2),
        offset[0].transpose(1, 0, 2), srow.transpose(1, 0, 2), scol.transpose(1, 0, 2),
        trow.transpose(1, 0, 2), tcol.transpose(1, 0, 2), count,
    )
    vmem = pl.BlockSpec(memory_space=pltpu.VMEM)
    dma = pltpu.SemaphoreType.DMA
    f32 = jnp.float32
    out = pl.pallas_call(
        functools.partial(kernel, n_sec, n_tile),
        out_shape=jax.ShapeDtypeStruct((2, nodes_hi, LANES), f32),
        in_specs=[pl.BlockSpec(memory_space=pltpu.HBM)] * 9,
        out_specs=vmem,
        scratch_shapes=[
            pltpu.VMEM((2, nodes_hi, LANES), f32),
            pltpu.VMEM((nodes_hi, LANES), f32),
            pltpu.VMEM((3, 1, slots), f32),
            pltpu.VMEM((2, 3, 2, slots), f32),
            pltpu.VMEM((2, 3, 1, slots), jnp.int32),
            pltpu.VMEM((2, 3, 1, slots), jnp.int32),
            pltpu.VMEM((1, 3), jnp.int32),
            dma((9,)),
            pltpu.VMEM((2, rows, chunks, LANES), f32),
            pltpu.VMEM((2, rows, chunks, LANES), f32),
            pltpu.VMEM((rows, chunks, LANES), f32),
            pltpu.VMEM((rows, chunks, LANES), f32),
            pltpu.VMEM((2, LANES, 3 * slots), jnp.bfloat16),
            pltpu.VMEM((2, nodes_hi, 3 * slots), jnp.bfloat16),
            pltpu.VMEM((2, 3, 1, slots), jnp.int32),
            pltpu.VMEM((STEPS, 2, 3, chunks, LANES), f32),
            pltpu.VMEM((STEPS, 2, 3, chunks, LANES), f32),
            pltpu.VMEM((STEPS, 2, 3, 2, slots), f32),
            pltpu.VMEM((STEPS, 2, 3, 2, slots), f32),
            pltpu.VMEM((2, 3, 1, slots), f32),
            dma((STEPS, 2, 3)),
            dma((STEPS, 2, 3)),
            dma((STEPS, 2, 3)),
            dma((STEPS, 2, 3)),
            dma((3,)),
            dma((3,)),
        ],
        compiler_params=pltpu.CompilerParams(
            collective_id=0, has_side_effects=True, vmem_limit_bytes=24 * 1024 * 1024
        ),
    )(*[pltpu.with_memory_space_constraint(x, pltpu.HBM) for x in operands])
    out = out.reshape(2, chunks, rows, LANES).transpose(0, 2, 1, 3)
    return out.reshape(1, 2, rows, width)


def solution(mesh):
    placed = (
        P("sec", None, "tile", None),
        P("sec", "tile", None),
        P("sec", "tile", None),
        P("sec", None, "tile", None),
        P("sec", "tile", None),
        P("sec", "tile", None),
        P("sec", "tile", None),
        P("sec", "tile", None),
        P("sec", "tile"),
    )
    return jax.shard_map(
        functools.partial(relax, mesh.shape["sec"], mesh.shape["tile"]),
        mesh=mesh, in_specs=placed, out_specs=P("sec", None, "tile", None), check_vma=False,
    )
```

```python
import functools
import jax
import jax.numpy as jnp
from jax import lax
from jax.experimental import pallas as pl
from jax.experimental.pallas import tpu as pltpu
from jax.sharding import PartitionSpec as P

STEPS = 2
DAMPING = 0.7
LANES = 128
MESH = pl.DeviceIdType.MESH


def stencil(rows, above, below):
    chunks = rows[0].shape[0]
    lane = lax.broadcasted_iota(jnp.int32, rows[0].shape, 1)
    chunk = lax.broadcasted_iota(jnp.int32, rows[0].shape, 0)
    sums = []
    for here, beside in ((rows[0], above + rows[1]), (rows[1], rows[0] + below)):
        both = here + 0.5 * beside
        left = pltpu.roll(both, 1, 1)
        left = jnp.where(lane == 0, jnp.where(chunk == 0, 0.0, pltpu.roll(left, 1, 0)), left)
        right = pltpu.roll(both, LANES - 1, 1)
        right = jnp.where(
            lane == LANES - 1,
            jnp.where(chunk == chunks - 1, 0.0, pltpu.roll(right, chunks - 1, 0)),
            right,
        )
        sums.append(beside + left + right)
    return sums


def two_parts(values):
    high = values.astype(jnp.bfloat16)
    low = (values - high.astype(jnp.float32)).astype(jnp.bfloat16)
    return high, low


def kernel(
    n_sec, n_tile, disp_in, stiff_in, wgt_in, off_in, srow_in, scol_in, trow_in, tcol_in, cnt_in,
    out,
    disp, stiff, wgt, off, rows, cols, cnt, load_sem,
    field, force, total, inv, lhs, hot_lo, hot_hi, hi_ids, edge, halo, mine, theirs, weights,
    edge_send, edge_recv, val_send, val_recv, wgt_send, wgt_recv,
):
    sec = lax.axis_index("sec")
    tile = lax.axis_index("tile")
    chunks = field.shape[2]
    nodes_hi = 2 * chunks
    slots = wgt.shape[2]
    has_tile = [tile > 0, None, tile < n_tile - 1]
    first_role = jnp.where(sec < n_sec - 1, 0, 1)
    end_role = jnp.where(sec > 0, 2, 1)
    sides = ((0, 0), (2, 1))

    def when_tile(g, body):
        if has_tile[g] is None:
            body()
        else:
            pl.when(has_tile[g])(body)

    def each_role(body):
        def turn(role, carry):
            body(role)
            return carry

        lax.fori_loop(first_role, end_role, turn, jnp.int32(0))

    barrier = pltpu.get_barrier_semaphore()

    def greet(s, t):
        pl.semaphore_signal(barrier, inc=1, device_id=(s, t), device_id_type=MESH)

    for g in (0, 2):
        when_tile(g, lambda g=g: greet(sec, tile + g - 1))
    def greet_role(role):
        for g in (0, 2, 1):
            when_tile(g, lambda g=g: greet(sec + 1 - 2 * role, tile + g - 1))

    each_role(greet_role)

    low_side = jnp.where(tile > 0, 1, 0)
    high_side = jnp.where(tile < n_tile - 1, 1, 0)
    secs = jnp.where(sec > 0, 1, 0) + jnp.where(sec < n_sec - 1, 1, 0)
    greetings = low_side + high_side + secs * (1 + low_side + high_side)

    loads = [
        pltpu.make_async_copy(source, target, load_sem.at[i])
        for i, (source, target) in enumerate(
            (
                (disp_in, disp),
                (stiff_in, stiff),
                (scol_in, cols.at[0]),
                (srow_in, rows.at[0]),
                (tcol_in, cols.at[1]),
                (trow_in, rows.at[1]),
                (off_in, off.at[0]),
                (wgt_in, wgt),
                (cnt_in, cnt),
            )
        )
    ]
    for load in loads:
        load.start()

    def edge_copy(step, side, k, landed=False):
        to_side = side if landed else 1 - side
        return pltpu.make_async_remote_copy(
            src_ref=edge.at[step, side, k],
            dst_ref=halo.at[step, to_side, k],
            send_sem=edge_send.at[step, side, k],
            recv_sem=edge_recv.at[step, to_side, k],
            device_id=(sec, tile + 2 * side - 1),
            device_id_type=MESH,
        )

    def value_copy(step, role, g, landed=False):
        to_role, to_g = (role, g) if landed else (1 - role, 2 - g)
        return pltpu.make_async_remote_copy(
            src_ref=mine.at[step, role, g],
            dst_ref=theirs.at[step, to_role, to_g],
            send_sem=val_send.at[step, role, g],
            recv_sem=val_recv.at[step, to_role, to_g],
            device_id=(sec + 1 - 2 * role, tile + g - 1),
            device_id_type=MESH,
        )

    def weight_copy(g, landed=False):
        role = 1 if landed else 0
        to_g = g if landed else 2 - g
        return pltpu.make_async_remote_copy(
            src_ref=weights.at[0, g],
            dst_ref=weights.at[1, to_g],
            send_sem=wgt_send.at[g],
            recv_sem=wgt_recv.at[to_g],
            device_id=(sec + 1 - 2 * role, tile + g - 1),
            device_id_type=MESH,
        )

    def send_edges(step, k):
        for g, side in sides:
            pl.when(has_tile[g])(lambda side=side: edge_copy(step, side, k).start())

    def await_edges(step, k):
        for g, side in sides:
            pl.when(has_tile[g])(lambda side=side: edge_copy(step, side, k, True).wait_recv())

    for g, side in sides:

        @pl.when(jnp.logical_not(has_tile[g]))
        def _(g=g, side=side):
            halo[:, side] = jnp.zeros((STEPS,) + halo.shape[2:], jnp.float32)
            for role in range(2):
                weights[role, g] = jnp.zeros(weights.shape[2:], jnp.float32)
                for step in range(STEPS):
                    theirs[step, role, g] = jnp.zeros(theirs.shape[3:], jnp.float32)

    lane_slot = lax.broadcasted_iota(jnp.int32, (1, slots), 1)
    lo_node = lax.broadcasted_iota(jnp.int32, (LANES, slots), 0)
    hi_node = lax.broadcasted_iota(jnp.int32, (nodes_hi, slots), 0)

    loads[0].wait()
    loads[1].wait()
    for r in range(2):
        c_row = stiff[pl.ds(r, chunks, stride=2), :]
        edge[0, r, 2] = c_row
        for k in range(2):
            u_row = disp[k, pl.ds(r, chunks, stride=2), :]
            field[k, r] = u_row
            edge[0, r, k] = c_row * u_row

    for load in loads[2:]:
        load.wait()

    off[1] = jnp.zeros(off.shape[1:], jnp.float32)

    @pl.when(sec < n_sec - 1)
    def _():
        for g in range(3):

            def mask(g=g):
                weights[0, g] = jnp.where(lane_slot < cnt[:, g : g + 1], wgt[g], 0.0)

            when_tile(g, mask)

    def prepare(role):
        for g in range(3):
            col = cols[role, g]
            hi = rows[role, g] * chunks + (col >> 7)
            hi_ids[role, g] = hi
            at = pl.ds(g * slots, slots)
            hot = jnp.where(lo_node == (col & (LANES - 1)), 1.0, 0.0).astype(jnp.bfloat16)
            hot_lo[role, pl.ds(0, LANES), at] = hot
            hot_lo[role, pl.ds(LANES, LANES), at] = hot
            hot_hi[role, :, at] = jnp.where(hi_node == hi, 1.0, 0.0).astype(jnp.bfloat16)

    each_role(prepare)

    def pick(step, role):
        for g in (0, 2, 1):
            found = jnp.dot(
                lhs[...],
                hot_lo[role, :, pl.ds(g * slots, slots)],
                preferred_element_type=jnp.float32,
            )
            hit = hi_node == hi_ids[role, g]
            for k in range(2):
                value = jnp.sum(
                    jnp.where(hit, found[k * nodes_hi : (k + 1) * nodes_hi], 0.0),
                    axis=0,
                    keepdims=True,
                )
                mine[step, role, g, pl.ds(k, 1), :] = value - off[role, g, pl.ds(k, 1), :]

    def send_values(step, role):
        for g in (0, 2, 1):
            when_tile(g, lambda g=g: value_copy(step, role, g).start())

    def spread(role, g, values):
        at = pl.ds(g * slots, slots)
        high = [row.astype(jnp.bfloat16) for row in values]
        low = [(row - h.astype(jnp.float32)).astype(jnp.bfloat16) for row, h in zip(values, high)]
        summed = lax.dot_general(
            jnp.concatenate([hot_hi[role, :, at] * part for part in high + low], axis=0),
            hot_lo[role, pl.ds(0, LANES), at],
            (((1,), (1,)), ((), ())),
            preferred_element_type=jnp.float32,
        )
        half = len(values) * nodes_hi
        return summed[:half] + summed[half:]

    def drain(step):
        def drain_role(role):
            for g in range(3):
                when_tile(g, lambda g=g: value_copy(step, role, g).wait_send())

        each_role(drain_role)
        if step == 0:

            @pl.when(sec < n_sec - 1)
            def _():
                for g in range(3):
                    when_tile(g, lambda g=g: weight_copy(g).wait_send())

        for g, side in sides:

            @pl.when(has_tile[g])
            def _(side=side):
                for k in range(3 if step == 0 else 2):
                    edge_copy(step, side, k).wait_send()

    for step in range(STEPS):
        for k in range(2):
            part = two_parts(field[k].reshape(nodes_hi, LANES))
            lhs[pl.ds(k * nodes_hi, nodes_hi), pl.ds(0, LANES)] = part[0]
            lhs[pl.ds(k * nodes_hi, nodes_hi), pl.ds(LANES, LANES)] = part[1]
        each_role(functools.partial(pick, step))
        if step == 0:
            pl.semaphore_wait(barrier, greetings)
        each_role(functools.partial(send_values, step))
        if step == 0:

            @pl.when(sec < n_sec - 1)
            def _():
                for g in (0, 2, 1):
                    when_tile(g, lambda g=g: weight_copy(g).start())

            send_edges(0, 0)
            send_edges(0, 2)
        send_edges(step, 1)
        if step > 0:
            drain(step - 1)

        if step == 0:
            inv[...] = jnp.zeros(inv.shape, jnp.float32)

        force[...] = jnp.zeros(force.shape, jnp.float32)

        def spread_pulls(role, step=step):
            for batch in ((1, 0, 2),):
                if step == 0:

                    @pl.when(role == 1)
                    def _(batch=batch):
                        for g in batch:
                            when_tile(g, lambda g=g: weight_copy(g, True).wait_recv())

                for g in batch:
                    when_tile(g, lambda g=g: value_copy(step, role, g, True).wait_recv())
                at = 0.0
                for g in batch:
                    weight = weights[role, g]
                    pull = weight * (theirs[step, role, g] - mine[step, role, g])
                    values = [pull[0:1], pull[1:2]] + ([weight] if step == 0 else [])
                    at = at + spread(role, g, values)
                force[...] += at[: 2 * nodes_hi].reshape(force.shape)
                if step == 0:
                    inv[...] += at[2 * nodes_hi :].reshape(inv.shape)

        each_role(spread_pulls)

        if step == 0:
            await_edges(0, 2)
            c_rows = [edge[0, r, 2] for r in range(2)]
            sums = stencil(c_rows, halo[0, 0, 2], halo[0, 1, 2])
            for r in range(2):
                springs = c_rows[r] * sums[r]
                total[r] = springs
                inv[r] = DAMPING / (inv[r] + springs)

        for k in range(2):
            await_edges(step, k)
            sums = stencil([edge[step, r, k] for r in range(2)], halo[step, 0, k], halo[step, 1, k])
            for r in range(2):
                c_row = edge[0, r, 2]
                here = field[k, r]
                pulled = force[k, r] + c_row * sums[r] - here * total[r]
                new = here + pulled * inv[r]
                if step < STEPS - 1:
                    field[k, r] = new
                    edge[step + 1, r, k] = c_row * new
                else:
                    out[k, pl.ds(r, chunks, stride=2), :] = new
            if step < STEPS - 1 and k == 0:
                send_edges(step + 1, 0)

    drain(STEPS - 1)


def relax(n_sec, n_tile, *args):
    displacement, stiffness, weight, offset, srow, scol, trow, tcol, count = args
    rows, width = stiffness.shape[1:]
    slots = weight.shape[2]
    chunks = width // LANES
    nodes_hi = rows * chunks

    def interleaved(x):
        x = x.reshape(-1, rows, chunks, LANES).transpose(0, 2, 1, 3)
        return x.reshape(-1, nodes_hi, LANES)

    operands = (
        interleaved(displacement), interleaved(stiffness)[0], weight.transpose(1, 0, 2),
        offset[0].transpose(1, 0, 2), srow.transpose(1, 0, 2), scol.transpose(1, 0, 2),
        trow.transpose(1, 0, 2), tcol.transpose(1, 0, 2), count,
    )
    vmem = pl.BlockSpec(memory_space=pltpu.VMEM)
    dma = pltpu.SemaphoreType.DMA
    f32 = jnp.float32
    out = pl.pallas_call(
        functools.partial(kernel, n_sec, n_tile),
        out_shape=jax.ShapeDtypeStruct((2, nodes_hi, LANES), f32),
        in_specs=[pl.BlockSpec(memory_space=pltpu.HBM)] * 9,
        out_specs=vmem,
        scratch_shapes=[
            pltpu.VMEM((2, nodes_hi, LANES), f32),
            pltpu.VMEM((nodes_hi, LANES), f32),
            pltpu.VMEM((3, 1, slots), f32),
            pltpu.VMEM((2, 3, 2, slots), f32),
            pltpu.VMEM((2, 3, 1, slots), jnp.int32),
            pltpu.VMEM((2, 3, 1, slots), jnp.int32),
            pltpu.VMEM((1, 3), jnp.int32),
            dma((9,)),
            pltpu.VMEM((2, rows, chunks, LANES), f32),
            pltpu.VMEM((2, rows, chunks, LANES), f32),
            pltpu.VMEM((rows, chunks, LANES), f32),
            pltpu.VMEM((rows, chunks, LANES), f32),
            pltpu.VMEM((2 * nodes_hi, 2 * LANES), jnp.bfloat16),
            pltpu.VMEM((2, 2 * LANES, 3 * slots), jnp.bfloat16),
            pltpu.VMEM((2, nodes_hi, 3 * slots), jnp.bfloat16),
            pltpu.VMEM((2, 3, 1, slots), jnp.int32),
            pltpu.VMEM((STEPS, 2, 3, chunks, LANES), f32),
            pltpu.VMEM((STEPS, 2, 3, chunks, LANES), f32),
            pltpu.VMEM((STEPS, 2, 3, 2, slots), f32),
            pltpu.VMEM((STEPS, 2, 3, 2, slots), f32),
            pltpu.VMEM((2, 3, 1, slots), f32),
            dma((STEPS, 2, 3)),
            dma((STEPS, 2, 3)),
            dma((STEPS, 2, 3)),
            dma((STEPS, 2, 3)),
            dma((3,)),
            dma((3,)),
        ],
        compiler_params=pltpu.CompilerParams(
            collective_id=0, has_side_effects=True, vmem_limit_bytes=24 * 1024 * 1024
        ),
    )(*[pltpu.with_memory_space_constraint(x, pltpu.HBM) for x in operands])
    out = out.reshape(2, chunks, rows, LANES).transpose(0, 2, 1, 3)
    return out.reshape(1, 2, rows, width)


def solution(mesh):
    placed = (
        P("sec", None, "tile", None),
        P("sec", "tile", None),
        P("sec", "tile", None),
        P("sec", None, "tile", None),
        P("sec", "tile", None),
        P("sec", "tile", None),
        P("sec", "tile", None),
        P("sec", "tile", None),
        P("sec", "tile"),
    )
    return jax.shard_map(
        functools.partial(relax, mesh.shape["sec"], mesh.shape["tile"]),
        mesh=mesh, in_specs=placed, out_specs=P("sec", None, "tile", None), check_vma=False,
    )
```
